32 devices in a mesh: member: 4 (over z), lat: 8 (over y, x, core).
Axes of the slice: x: 2, y: 2, z: 4, core: 2. Of those that a mesh axis runs over, the one named last changes fastest.
Arguments:
- ensemble_state: float32 [3, 256, 64, 256], P(None, 'member', 'lat'), may hold values from -6 to 6
- obs_cell: int32 [8, 4, 256], replicated, may hold values from 0 to 511
- obs_value: float32 [8, 4, 256], replicated, may hold values from -6 to 6
- obs_prec: float32 [8, 4, 256], replicated, may hold values from 0.5 to 4
Outputs:
- analysis_a: float32 [3, 256, 64, 256], P(None, 'member', 'lat')
The draws below stay inside these ranges and needn't reach their ends.
Inputs may be any that keep to these rules, and one draw needn't show every extreme that they name: `obs_cell`: each entry is a cell of its patch of 8 by 64 cells, counted row by row.
All inputs are finite; a program needn't handle non-finite values.
Results may differ from the reference program's by a relative error of at most 0.0003.
Values sent between devices are 32-bit elements; how exact they have to be, the bound alone decides.
No kernel may reach another device: no remote copies, remote signals or barrier semaphores. Data moves between devices by JAX's collectives and lax.ppermute only.
A program may use at most 128 MiB of HBM per device.

```python
import math
import jax
import jax.numpy as jnp
from jax import lax

BAND_GRID_ROWS = 8
NLON = 256
OBS_P = 256
ITERS = 12
STEPS = 2
ENSEMBLE_SIZE = 256
NLAT = 64
PLON = 64
N_MEMBER = 4
N_LAT = 8


def place_ends(values, stream_key, least, high):
    place = [jax.random.randint(jax.random.fold_in(stream_key, axis), (), 0, length) for axis, length in enumerate(values.shape)]
    main_axis = values.shape.index(max(values.shape))
    next_to = place[:main_axis] + [(place[main_axis] + 1) % values.shape[main_axis]] + place[main_axis + 1:]
    return values.at[tuple(place)].set(least).at[tuple(next_to)].set(high)


def levels(own_key, dims, shards, smallest, largest):
    def one(axis_at, blocks):
        draws = jax.random.uniform(jax.random.fold_in(jax.random.fold_in(own_key, 6), axis_at), (blocks,), jnp.float32, smallest / len(shards), largest / len(shards))
        return jnp.repeat(jnp.exp(draws), dims[axis_at] // blocks).reshape((-1,) + (1,) * (len(dims) - axis_at - 1))

    loudness = one(*shards[0])
    for cut in shards[1:]:
        loudness = loudness * one(*cut)
    return loudness


def noise(stream_key, dims, scale, most, cuts=(), held_as=jnp.bfloat16):
    level = levels(stream_key, dims, cuts, -0.22, 0.18) if cuts else 1.0
    entries = jax.random.normal(stream_key, dims, jnp.float32) * scale * level
    return jnp.minimum(jnp.maximum(entries, -most), most).astype(held_as)


def setup_inputs(seed: int = 0) -> dict:
    arg_keys = jax.random.split(jax.random.key(seed), 5)
    ensemble_state = noise(arg_keys[0], (3, ENSEMBLE_SIZE, NLAT, NLON), 1.0, 6.0, ((1, 4), (2, 8)), jnp.float32)
    obs_cell = place_ends(jax.random.randint(arg_keys[1], (N_LAT, N_MEMBER, OBS_P), 0, BAND_GRID_ROWS * PLON), jax.random.fold_in(arg_keys[1], 1), 0, (BAND_GRID_ROWS * PLON) - 1).astype(jnp.int32)
    obs_value = noise(arg_keys[2], (N_LAT, N_MEMBER, OBS_P), 1.0, 6.0, (), jnp.float32)
    obs_prec = jnp.clip(jnp.exp(jax.random.uniform(arg_keys[3], (N_LAT, N_MEMBER, OBS_P), jnp.float32, math.log(0.5), math.log(4.0))), 0.5, 4.0)
    return dict(ensemble_state=ensemble_state, obs_cell=obs_cell, obs_value=obs_value, obs_prec=obs_prec)


time_step = 0.3
coriolis_base = 0.5
coriolis_slope = 1.0

def planetary(row_ids, total_rows):
    return coriolis_base + coriolis_slope * (row_ids / total_rows - 0.5)

def along_lon(model_field):
    inner = jnp.pad(model_field[:, 1:-1, :], ((0, 0), (0, 0), (1, 1)))
    return 0.5 * (inner[:, :, 2:] - inner[:, :, :-2])

def along_lat(model_field):
    return 0.5 * (model_field[:, 2:, :] - model_field[:, :-2, :])

def tendency(padded, spinup_rows):
    height, zonal, meridional = (padded[0], padded[1], padded[2])
    spin = spinup_rows[None, :, None]
    height_rate = -(along_lon(zonal) + along_lat(meridional))
    zonal_rate = -along_lon(height) + spin * meridional[:, 1:-1, :]
    merid_rate = -along_lat(height) - spin * zonal[:, 1:-1, :]
    return jnp.stack([height_rate, zonal_rate, merid_rate])

def advance_model(model_state, spinup_rows, widen_band):
    for sweep in range(STEPS):
        first_rate = tendency(widen_band(model_state), spinup_rows)
        midpoint = model_state + time_step * first_rate
        second_rate = tendency(widen_band(midpoint), spinup_rows)
        model_state = model_state + 0.5 * time_step * (first_rate + second_rate)
    return model_state

def analyse(blocks, near_values, near_precs, near_cells, states, lat_index, lon_index, section_width, band_rows):
    members = blocks.shape[2]
    highest = lax.Precision.HIGHEST
    offsets = jnp.arange(3, dtype=jnp.int32) - 1
    obs_mean = lax.optimization_barrier(jnp.mean(blocks, axis=2))
    deviation = blocks - obs_mean[:, :, None, :]
    innovation = near_values - obs_mean
    obs_row = (offsets[:, None, None] * band_rows + near_cells // section_width).astype(jnp.float32)
    obs_col = (offsets[None, :, None] * section_width + near_cells % section_width).astype(jnp.float32)
    north = (obs_row - 0.5 * (band_rows - 1)) / band_rows
    east = (obs_col - 0.5 * (section_width - 1)) / section_width
    taper = jnp.exp(-0.5 * (north * north + east * east))
    weight = near_precs * taper
    scaled = deviation * weight[:, :, None, :]
    identity = jnp.eye(members, dtype=jnp.float32)
    gram_matrix = jnp.einsum('abko,abjo->kj', scaled, deviation, precision=highest) + (members - 1.0) * identity
    drive_vec = jnp.einsum('abko,abo->k', scaled, innovation, precision=highest)
    fro_norm = jnp.sqrt(jnp.sum(gram_matrix * gram_matrix))
    root_iter = gram_matrix / fro_norm
    inverse = identity
    for sweep in range(ITERS):
        correction = 1.5 * identity - 0.5 * jnp.dot(inverse, root_iter, precision=highest)
        root_iter = jnp.dot(root_iter, correction, precision=highest)
        inverse = jnp.dot(correction, inverse, precision=highest)
    mean_weight = jnp.dot(inverse, jnp.dot(inverse, drive_vec, precision=highest), precision=highest) / fro_norm
    weights = jnp.sqrt(members - 1.0) / jnp.sqrt(fro_norm) * inverse + mean_weight[:, None]
    state_mean = lax.optimization_barrier(jnp.mean(states, axis=1, keepdims=True))
    return state_mean + jnp.einsum('jk,fjc->fkc', weights, states - state_mean, precision=highest)

def reference(ensemble_state, obs_cell, obs_value, obs_prec):
    section_width = NLON // N_MEMBER
    spinup_rows = planetary(jnp.arange(NLAT, dtype=jnp.float32), NLAT)

    def widen_band(model_field):
        return jnp.pad(model_field, ((0, 0), (0, 0), (1, 1), (0, 0)))
    advance_model_alt = advance_model(ensemble_state, spinup_rows, widen_band)
    local_patches = advance_model_alt.reshape(3, ENSEMBLE_SIZE, N_LAT, BAND_GRID_ROWS, N_MEMBER, section_width)
    local_patches = local_patches.transpose(2, 4, 0, 1, 3, 5).reshape(N_LAT, N_MEMBER, 3, ENSEMBLE_SIZE, BAND_GRID_ROWS * section_width)
    heights = local_patches[:, :, 0]
    where_obs = jnp.broadcast_to(obs_cell[:, :, None, :], (N_LAT, N_MEMBER, ENSEMBLE_SIZE, OBS_P))
    observed = jnp.take_along_axis(heights, where_obs, axis=3)
    padded_obs = jnp.pad(observed, ((1, 1), (1, 1), (0, 0), (0, 0)))
    padded_values = jnp.pad(obs_value, ((1, 1), (1, 1), (0, 0)))
    padded_precs = jnp.pad(obs_prec, ((1, 1), (1, 1), (0, 0)))
    padded_cells = jnp.pad(obs_cell, ((1, 1), (1, 1), (0, 0)))

    def analyse_patch(patch_id):
        zero_index = jnp.zeros((), jnp.int32)
        lat_index = (patch_id // N_MEMBER).astype(jnp.int32)
        lon_index = (patch_id % N_MEMBER).astype(jnp.int32)
        blocks = lax.dynamic_slice(padded_obs, (lat_index, lon_index, zero_index, zero_index), (3, 3, ENSEMBLE_SIZE, OBS_P))
        near_values = lax.dynamic_slice(padded_values, (lat_index, lon_index, zero_index), (3, 3, OBS_P))
        near_precs = lax.dynamic_slice(padded_precs, (lat_index, lon_index, zero_index), (3, 3, OBS_P))
        near_cells = lax.dynamic_slice(padded_cells, (lat_index, lon_index, zero_index), (3, 3, OBS_P))
        states = local_patches[lat_index, lon_index]
        return analyse(blocks, near_values, near_precs, near_cells, states, lat_index, lon_index, section_width, BAND_GRID_ROWS)
    analysed = lax.map(analyse_patch, jnp.arange(N_LAT * N_MEMBER, dtype=jnp.int32))
    analysed = analysed.reshape(N_LAT, N_MEMBER, 3, ENSEMBLE_SIZE, BAND_GRID_ROWS, section_width)
    analysis_a = analysed.transpose(2, 3, 0, 4, 1, 5).reshape(3, ENSEMBLE_SIZE, NLAT, NLON)
    return analysis_a
```

```python
import functools

import jax
import jax.numpy as jnp
from jax import lax
from jax.experimental import pallas as pl
from jax.experimental.pallas import tpu as pltpu
from jax.sharding import PartitionSpec as P

ITERS = 12
STEPS = 2
HALO = 2 * STEPS
LANES = 128

time_step = 0.3
coriolis_base = 0.5
coriolis_slope = 1.0

F32 = jnp.float32
BF16 = jnp.bfloat16


def call(kernel, outs, *args, name, flops=0, limit=24, far_in=False, far_out=False):
    shapes = [jax.ShapeDtypeStruct(s, F32) for s in outs[0]]
    spaces = [pl.ANY if far else pltpu.VMEM for far in (far_in, far_out)]
    bytes_moved = sum(a.size * 4 for a in args) + sum(s.size * 4 for s in shapes)
    return pl.pallas_call(
        kernel,
        out_shape=shapes,
        in_specs=[pl.BlockSpec(memory_space=spaces[0])] * len(args),
        out_specs=[pl.BlockSpec(memory_space=spaces[1])] * len(shapes),
        scratch_shapes=outs[1],
        compiler_params=pltpu.CompilerParams(vmem_limit_bytes=limit * 2**20),
        cost_estimate=pl.CostEstimate(flops=flops, bytes_accessed=bytes_moved, transcendentals=0),
        name=name,
    )(*args)


def split(x):
    high = x.astype(BF16)
    return high, (x - high.astype(F32)).astype(BF16)


def dot3(a, b, dims=(((1,), (0,)), ((), ()))):
    ah, al = a
    bh, bl = b
    dot = functools.partial(lax.dot_general, dimension_numbers=dims, preferred_element_type=F32)
    return dot(ah, bh) + (dot(ah, bl) + dot(al, bh))


def model_kernel(source, own, h_pair, h_cross, uv_pair, uv_cross, state, sems):
    _, rows, members, lon = own.shape
    tiles = lon // LANES
    copies = [
        pltpu.make_async_copy(source.at[:, :, pl.ds(t * LANES, LANES)], state.at[t], sems.at[t])
        for t in range(tiles)
    ]
    for copy in copies:
        copy.start()
    lat = lax.axis_index("lat")
    size = lax.axis_size("lat")
    even = lat % 2 == 0
    inside_up = (lat > 0).astype(F32)
    inside_down = (lat < size - 1).astype(F32)
    total = float(rows * size)
    lane = lax.broadcasted_iota(jnp.int32, (8, LANES), 1)
    first, last = lane == 0, lane == LANES - 1
    spins = [
        coriolis_base + coriolis_slope * ((lat * rows + r).astype(F32) / total - 0.5)
        for r in range(-HALO, rows + HALO)
    ]

    def diff_lon(x):
        right = [pltpu.roll(t, 1, 1) for t in x]
        left = [pltpu.roll(t, LANES - 1, 1) for t in x]
        out = []
        for t in range(tiles):
            before = jnp.where(first, right[t - 1] if t else 0.0, right[t])
            after = jnp.where(last, left[t + 1] if t + 1 < tiles else 0.0, left[t])
            out.append(after - before)
        return out

    def block(b, _):
        start = pl.multiple_of(b * 8, 8)

        def load(f, r):
            return [
                state[t, f, pl.ds(start * rows + r, 8, stride=rows), :]
                for t in range(tiles)
            ]

        base = {r: [load(f, r) for f in range(3)] for r in range(rows)}
        y = dict(base)
        for step, factor in enumerate((time_step / 4, time_step / 2, time_step, 2 * time_step)):
            new = {}
            for r in range(-step - 1, rows + step + 1):
                scale = factor
                if r < 0:
                    scale = factor * inside_up
                elif r >= rows:
                    scale = factor * inside_down
                half = 0.5 * scale
                turn = scale * spins[r + HALO]
                here, below, above = y.get(r), y.get(r - 1), y.get(r + 1)
                rates = [[None] * tiles for _ in range(3)]

                def add(f, t, term):
                    rates[f][t] = term if rates[f][t] is None else rates[f][t] + term

                if here is not None:
                    slope_h, slope_u = diff_lon(here[0]), diff_lon(here[1])
                for t in range(tiles):
                    d_v = d_h = None
                    if above is not None and below is not None:
                        d_h, d_v = above[0][t] - below[0][t], above[2][t] - below[2][t]
                    elif above is not None:
                        d_h, d_v = above[0][t], above[2][t]
                    elif below is not None:
                        d_h, d_v = -below[0][t], -below[2][t]
                    if here is not None:
                        d_v = slope_u[t] if d_v is None else d_v + slope_u[t]
                        add(1, t, turn * here[2][t] - half * slope_h[t])
                    if d_v is not None:
                        add(0, t, -half * d_v)
                    if d_h is not None:
                        add(2, t, -half * d_h)
                    if here is not None:
                        add(2, t, -turn * here[1][t])
                zero = jnp.zeros((8, LANES), F32)
                for f in range(3):
                    for t in range(tiles):
                        if r in base:
                            rates[f][t] = base[r][f][t] + rates[f][t]
                        elif rates[f][t] is None:
                            rates[f][t] = zero
                new[r] = rates
            y = new
        at = pl.ds(start, 8)
        for t in range(tiles):
            cols = pl.ds(t * LANES, LANES)
            for r in range(rows):
                for f in range(3):
                    own[f, r, at, cols] = y[r][f][t]
            for i in range(HALO):
                up, down = y[i - HALO], y[rows + i]
                h_pair[i, at, cols] = jnp.where(even, down[0][t], up[0][t])
                h_cross[i, at, cols] = jnp.where(even, up[0][t], down[0][t])
                for f in range(2):
                    uv_pair[f, i, at, cols] = jnp.where(even, down[f + 1][t], up[f + 1][t])
                    uv_cross[f, i, at, cols] = jnp.where(even, up[f + 1][t], down[f + 1][t])
        return 0

    for copy in copies:
        copy.wait()
    lax.fori_loop(0, members // 8, block, 0)


def halo_places(rows):
    even = lax.axis_index("lat") % 2 == 0
    pair = jnp.where(even, rows - HALO, 0)
    return pair, rows - HALO - pair


def observe_kernel(width, own, got_pair, got_cross, cells_row, cells_lane, raw, height):
    _, rows, members, lon = own.shape
    patches, _, n_obs = raw.shape
    pair, cross = halo_places(rows)
    height[...] = own[0]
    height[pl.ds(pair, HALO)] += got_pair[...]
    height[pl.ds(cross, HALO)] += got_cross[...]
    for q in range(patches):
        window = pl.ds(q * width // LANES * LANES, LANES)
        for c in range(0, n_obs, LANES):
            lane = jnp.broadcast_to(cells_lane[q, :, pl.ds(c, LANES)], (members, LANES))
            row = jnp.broadcast_to(cells_row[q, :, pl.ds(c, LANES)], (members, LANES))
            total = None
            for r in range(rows):
                taken = jnp.take_along_axis(height[r, :, window], lane, axis=1)
                total = taken if total is None else jnp.where(row == r, taken, total)
            raw[q, :, pl.ds(c, LANES)] = total


def pack_kernel(width, own, height, got_pair, got_cross, *outs):
    uv = outs[-1]
    outs = outs[:-1]
    _, rows, members, lon = own.shape
    pair, cross = halo_places(rows)
    uv[...] = own[1:3]
    for f in range(2):
        uv[f, pl.ds(pair, HALO)] += got_pair[f]
        uv[f, pl.ds(cross, HALO)] += got_cross[f]
    mine = lax.axis_index("member")
    n = len(outs)
    per = LANES // width
    slot = lax.broadcasted_iota(jnp.int32, (members, LANES), 1) // width
    for s, out in enumerate(outs):
        q = owner_of(mine, s, n)
        start = pl.multiple_of(q * width // LANES * LANES, LANES)
        offset = q * width - start
        for f in range(3):
            source = height if f == 0 else uv.at[f - 1]
            for r in range(0, rows, per):
                total = None
                for i in range(per):
                    line = source[r + i, :, pl.ds(start, LANES)]
                    line = pltpu.roll(line, lax.rem(i * width - offset + LANES, LANES), 1)
                    total = line if total is None else jnp.where(slot == i, line, total)
                out[:, pl.ds((f * rows + r) * width, LANES)] = total


def owner_of(mine, shift, n):
    if n & (n - 1) == 0:
        return mine ^ shift
    return lax.rem(mine + shift, n)


def source_of(mine, shift, n):
    if n & (n - 1) == 0:
        return mine ^ shift
    return lax.rem(mine - shift + n, n)


def swap_links(n, shift):
    return [(i, owner_of(i, shift, n) if n & (n - 1) == 0 else (i + shift) % n) for i in range(n)]


def neighbour_links(n, first):
    links = [(i, i + 1) for i in range(first, n - 1, 2)]
    return links + [(j, i) for i, j in links]


def centred(raw):
    mean = jnp.sum(raw, axis=0, keepdims=True) * (1.0 / raw.shape[0])
    return raw - mean, mean


def gram_kernel(targets, raw_own, raw_pair, raw_cross, weight, value, *outs):
    members, n_obs = raw_own.shape
    total = [None] * len(targets)
    for b, raw in enumerate((raw_own, raw_pair, raw_cross)):
        dev, mean = centred(raw[...])
        innovation = value[b : b + 1] - mean
        right = split(dev)
        for i, t in enumerate(targets):
            w = weight[t, b : b + 1]
            left = jnp.concatenate(
                [dev * w, jnp.broadcast_to(innovation * w, (16, n_obs))], axis=0
            )
            part = dot3(split(left), right, (((1,), (1,)), ((), ())))
            total[i] = part if total[i] is None else total[i] + part
    for out, t in zip(outs, total):
        out[...] = t


def weights_kernel(own, got_pair, got_cross, out):
    members = own.shape[1]
    rows = lax.broadcasted_iota(jnp.int32, (members, members), 0)
    cols = lax.broadcasted_iota(jnp.int32, (members, members), 1)
    diagonal = rows == cols
    at = pl.ds(0, members)
    gram = own[at] + got_pair[at] + got_cross[at]
    gram = gram + jnp.where(diagonal, members - 1.0, 0.0)
    at = pl.ds(members, 8)
    drive = own[at] + got_pair[at] + got_cross[at]
    square = jnp.sum(jnp.sum(gram * gram, axis=0, keepdims=True), axis=1, keepdims=True)
    fro = jnp.sqrt(square)
    root = gram / fro
    inverse = None
    for sweep in range(ITERS):
        root_s = split(root)
        if inverse is None:
            product = root
        else:
            inverse_s = split(inverse)
            product = dot3(inverse_s, root_s)
        correction = jnp.where(diagonal, 1.5, 0.0) - 0.5 * product
        correction_s = split(correction)
        if sweep + 1 < ITERS:
            root = dot3(root_s, correction_s)
        inverse = correction if inverse is None else dot3(correction_s, inverse_s)
    inverse_s = split(inverse)
    mean_weight = dot3(split(dot3(split(drive), inverse_s)), inverse_s)[0:1] / fro
    weights = jnp.sqrt(members - 1.0) / jnp.sqrt(fro) * inverse + mean_weight
    sums = jnp.sum(weights, axis=1, keepdims=True)
    out[...] = weights + (1.0 - sums) * (1.0 / members)


def apply_kernel(n, weights, *refs):
    parts, outs, whole = refs[:n], refs[n : 2 * n], refs[2 * n]
    members = weights.shape[0]
    local, cells = parts[0].shape
    mine = lax.axis_index("member")
    for s, part in enumerate(parts):
        whole[pl.ds(pl.multiple_of(source_of(mine, s, n) * local, local), local), :] = part[...]
    wide = 2 * LANES
    for c in range(0, cells, wide):
        at = pl.ds(c, wide)
        field = split(whole[:, at])
        for s, out in enumerate(outs):
            k = pl.multiple_of(source_of(mine, s, n) * local, local)
            out[:, at] = dot3(split(weights[pl.ds(k, local), :]), field)


def unpack_kernel(width, n, rows, *refs):
    parts, (out, whole, lines_out, sems) = refs[:n], refs[n:]
    members = parts[0].shape[0]
    mine = lax.axis_index("member")
    for s, part in enumerate(parts):
        whole[owner_of(mine, s, n)] = part[...]
    per = LANES // width
    slot = lax.broadcasted_iota(jnp.int32, (members, LANES), 1) // width
    copies = []
    for f in range(3):
        for r in range(0, rows, per):
            cols = pl.ds((f * rows + r) * width, LANES)
            for t in range(n // per):
                lines = [whole[t * per + i, :, cols] for i in range(per)]
                for j in range(per):
                    total = None
                    for i in range(per):
                        line = lines[i]
                        if i != j:
                            line = pltpu.roll(line, (i - j) * width % LANES, 1)
                        total = line if total is None else jnp.where(slot == i, line, total)
                    lines_out[t, f, pl.ds(r + j, members, stride=rows), :] = total
        for t in range(n // per):
            copies.append(
                pltpu.make_async_copy(
                    lines_out.at[t, f], out.at[f, :, pl.ds(t * LANES, LANES)], sems.at[t, f]
                )
            )
            copies[-1].start()
    for copy in copies:
        copy.wait()


def body(ensemble_state, obs_cell, obs_value, obs_prec):
    _, members, rows, lon = ensemble_state.shape
    n_lat, n_member = lax.axis_size("lat"), lax.axis_size("member")
    lat, mine = lax.axis_index("lat"), lax.axis_index("member")
    width = lon // n_member
    all_members = members * n_member
    patches, n_obs = obs_cell.shape[1:]
    zero = jnp.zeros((), jnp.int32)
    pair_lat, cross_lat = neighbour_links(n_lat, 0), neighbour_links(n_lat, 1)
    pair_lon, cross_lon = neighbour_links(n_member, 0), neighbour_links(n_member, 1)

    offsets = jnp.arange(3, dtype=jnp.int32) - 1

    def near(array):
        padded = jnp.pad(array, ((0, 0), (1, 1), (0, 0)))
        return lax.dynamic_slice(padded, (lat, mine, zero), (1, 3, n_obs))[0]

    def ordered(array, index, axis):
        low, middle, high = [lax.index_in_dim(array, i, axis, keepdims=True) for i in range(3)]
        even = index % 2 == 0
        return jnp.concatenate(
            [middle, jnp.where(even, high, low), jnp.where(even, low, high)], axis=axis
        )

    cells = near(obs_cell)
    obs_row = (-offsets[:, None, None] * rows + cells // width).astype(F32)
    obs_col = (offsets[:, None] * width + cells % width).astype(F32)
    north = (obs_row - 0.5 * (rows - 1)) / rows
    east = (obs_col - 0.5 * (width - 1)) / width
    weight = near(obs_prec) * jnp.exp(-0.5 * (north * north + east * east))
    weight = ordered(ordered(weight, mine, 1), lat, 0)
    value = ordered(near(obs_value), mine, 0)
    band = lax.dynamic_slice(obs_cell, (lat, zero, zero), (1, patches, n_obs))[0][:, None, :]
    starts = jnp.arange(patches, dtype=jnp.int32)[:, None, None] * width % LANES
    cells_row, cells_lane = band // width, band % width + starts

    edge = (HALO, members, lon)
    own, h_pair, h_cross, uv_pair, uv_cross = call(
        model_kernel,
        (
            [(3, rows, members, lon), edge, edge, (2,) + edge, (2,) + edge],
            [
                pltpu.VMEM((lon // LANES, 3, members * rows, LANES), F32),
                pltpu.SemaphoreType.DMA((lon // LANES,)),
            ],
        ),
        ensemble_state.reshape(3, members * rows, lon),
        name="model",
        far_in=True,
    )
    got_cross = lax.ppermute(h_cross, "lat", cross_lat)
    got_pair = lax.ppermute(h_pair, "lat", pair_lat)
    raw, height = call(
        functools.partial(observe_kernel, width),
        ([(patches, members, n_obs), (rows, members, lon)], []),
        own,
        got_pair,
        got_cross,
        cells_row,
        cells_lane,
        name="observe",
    )
    raw = lax.all_to_all(raw, "member", split_axis=0, concat_axis=0, tiled=True)
    raw = raw.reshape(all_members, n_obs)
    uv_cross, uv_pair = lax.ppermute(uv_cross, "lat", cross_lat), lax.ppermute(uv_pair, "lat", pair_lat)
    packed = call(
        functools.partial(pack_kernel, width),
        ([(members, 3 * rows * width)] * n_member, [pltpu.VMEM((2, rows, members, lon), F32)]),
        own,
        height,
        uv_pair,
        uv_cross,
        name="pack",
    )
    raw_cross = lax.ppermute(raw, "member", cross_lon)
    raw_pair = lax.ppermute(raw, "member", pair_lon)
    order = sorted(range(1, n_member), key=lambda s: (-(s & -s), s))
    parts = [packed[0]] + [None] * (n_member - 1)
    for s in order:
        parts[s] = lax.ppermute(packed[s], "member", swap_links(n_member, s))
    gram_shape = (all_members + 16, all_members)
    flops = 2 * 9 * all_members**2 * n_obs
    gram_cross, gram_pair = call(
        functools.partial(gram_kernel, (2, 1)),
        ([gram_shape] * 2, []),
        raw, raw_pair, raw_cross, weight, value,
        name="gram_beside", flops=2 * flops,
    )
    gram_cross = lax.ppermute(gram_cross, "lat", cross_lat)
    gram_pair = lax.ppermute(gram_pair, "lat", pair_lat)
    (gram_own,) = call(
        functools.partial(gram_kernel, (0,)),
        ([gram_shape], []),
        raw, raw_pair, raw_cross, weight, value,
        name="gram_own", flops=flops,
    )
    (weights,) = call(
        weights_kernel,
        ([(all_members, all_members)], []),
        gram_own, gram_pair, gram_cross,
        name="weights", flops=2 * 9 * 12 * all_members**3,
    )
    shape = packed[0].shape
    done = call(
        functools.partial(apply_kernel, n_member),
        ([shape] * n_member, [pltpu.VMEM((all_members, shape[1]), F32)]),
        weights, *parts,
        name="apply", flops=6 * all_members**2 * shape[1],
    )
    final = [done[0]] + [None] * (n_member - 1)
    for s in order:
        back = [(j, i) for i, j in swap_links(n_member, s)]
        final[s] = lax.ppermute(done[s], "member", back)
    (analysis,) = call(
        functools.partial(unpack_kernel, width, n_member, rows),
        (
            [(3, members * rows, lon)],
            [
                pltpu.VMEM((n_member,) + shape, F32),
                pltpu.VMEM((lon // LANES, 3, members * rows, LANES), F32),
                pltpu.SemaphoreType.DMA((lon // LANES, 3)),
            ],
        ),
        *final,
        name="unpack",
        far_out=True,
    )
    return analysis.reshape(ensemble_state.shape)


def solution(mesh):
    in_specs = (P(None, "member", "lat", None), P(), P(), P())
    out_specs = P(None, "member", "lat", None)
    return jax.shard_map(body, mesh=mesh, in_specs=in_specs, out_specs=out_specs, check_vma=False)
```

```python
import functools

import jax
import jax.numpy as jnp
from jax import lax
from jax.experimental import pallas as pl
from jax.experimental.pallas import tpu as pltpu
from jax.sharding import PartitionSpec as P

ITERS = 12
STEPS = 2
HALO = 2 * STEPS
LANES = 128
LIMIT = 12

time_step = 0.3
coriolis_base = 0.5
coriolis_slope = 1.0

F32 = jnp.float32
BF16 = jnp.bfloat16


def call(kernel, outs, *args, name, flops=0, limit=LIMIT):
    shapes = [jax.ShapeDtypeStruct(s, F32) for s in outs[0]]
    bytes_moved = 0
    return pl.pallas_call(
        kernel,
        out_shape=shapes,
        in_specs=[pl.BlockSpec(memory_space=pltpu.VMEM)] * len(args),
        out_specs=[pl.BlockSpec(memory_space=pltpu.VMEM)] * len(shapes),
        scratch_shapes=outs[1],
        compiler_params=pltpu.CompilerParams(vmem_limit_bytes=limit * 2**20),
        cost_estimate=pl.CostEstimate(flops=0, bytes_accessed=bytes_moved, transcendentals=0),
        name=name,
    )(*args)


def split(x):
    high = x.astype(BF16)
    return high, (x - high.astype(F32)).astype(BF16)


def dot3(a, b, dims=(((1,), (0,)), ((), ()))):
    ah, al = a
    bh, bl = b
    dot = functools.partial(lax.dot_general, dimension_numbers=dims, preferred_element_type=F32)
    return dot(ah, bh) + (dot(ah, bl) + dot(al, bh))


def coefficients(rows):
    lat, size = lax.axis_index("lat"), lax.axis_size("lat")
    inside_up = (lat > 0).astype(F32)
    inside_down = (lat < size - 1).astype(F32)
    inside = {r: inside_up if r < 0 else inside_down for r in range(-HALO, rows + HALO)}
    spins = {
        r: coriolis_base + coriolis_slope * ((lat * rows + r).astype(F32) / float(rows * size) - 0.5)
        for r in inside
    }
    return inside, spins


def integrate(base, diff_lon, keep, rows, inside, spins):
    tiles = len(base[0][0])
    y = dict(base)
    for step, factor in enumerate((time_step / 4, time_step / 2, time_step, 2 * time_step)):
        new = {}
        for r in range(-step - 1, rows + step + 1):
            scale = factor if 0 <= r < rows else factor * inside[r]
            half, turn = 0.5 * scale, scale * spins[r]
            if keep is not None:
                half, turn = half * keep, turn * keep
            here, below, above = y.get(r), y.get(r - 1), y.get(r + 1)
            rates = [[None] * tiles for _ in range(3)]

            def add(f, t, term):
                rates[f][t] = term if rates[f][t] is None else rates[f][t] + term

            if here is not None:
                slope_h, slope_u = diff_lon(here[0]), diff_lon(here[1])
            for t in range(tiles):
                d_v = d_h = None
                if above is not None and below is not None:
                    d_h, d_v = above[0][t] - below[0][t], above[2][t] - below[2][t]
                elif above is not None:
                    d_h, d_v = above[0][t], above[2][t]
                elif below is not None:
                    d_h, d_v = -below[0][t], -below[2][t]
                if here is not None:
                    d_v = slope_u[t] if d_v is None else d_v + slope_u[t]
                    add(1, t, turn * here[2][t] - half * slope_h[t])
                if d_v is not None:
                    add(0, t, -half * d_v)
                if d_h is not None:
                    add(2, t, -half * d_h)
                if here is not None:
                    add(2, t, -turn * here[1][t])
            for f in range(3):
                for t in range(tiles):
                    if r in base:
                        rates[f][t] = base[r][f][t] + rates[f][t]
                    elif rates[f][t] is None:
                        rates[f][t] = jnp.zeros((8, LANES), F32)
            new[r] = rates
        y = new
    return y


def model_kernel(state, own, h_pair, h_cross, uv_pair, uv_cross):
    _, rows, members, lon = own.shape
    tiles = lon // LANES
    even = lax.axis_index("lat") % 2 == 0
    inside, spins = coefficients(rows)
    lane = lax.broadcasted_iota(jnp.int32, (8, LANES), 1)
    first, last = lane == 0, lane == LANES - 1

    def diff_lon(x):
        right = [pltpu.roll(t, 1, 1) for t in x]
        left = [pltpu.roll(t, LANES - 1, 1) for t in x]
        out = []
        for t in range(tiles):
            before = jnp.where(first, right[t - 1] if t else 0.0, right[t])
            after = jnp.where(last, left[t + 1] if t + 1 < tiles else 0.0, left[t])
            out.append(after - before)
        return out

    def block(b, _):
        start = pl.multiple_of(b * 8, 8)

        def load(f, r):
            return [
                state[f, pl.ds((start * tiles + t) * rows + r, 8, stride=rows * tiles), :]
                for t in range(tiles)
            ]

        base = {r: [load(f, r) for f in range(3)] for r in range(rows)}
        y = integrate(base, diff_lon, None, rows, inside, spins)
        at = pl.ds(start, 8)
        for t in range(tiles):
            cols = pl.ds(t * LANES, LANES)
            for r in range(rows):
                for f in range(3):
                    own[f, r, at, cols] = y[r][f][t]
            for i in range(HALO):
                up, down = y[i - HALO], y[rows + i]
                h_pair[i, at, cols] = jnp.where(even, down[0][t], up[0][t])
                h_cross[i, at, cols] = jnp.where(even, up[0][t], down[0][t])
                for f in range(2):
                    uv_pair[f, i, at, cols] = jnp.where(even, down[f + 1][t], up[f + 1][t])
                    uv_cross[f, i, at, cols] = jnp.where(even, up[f + 1][t], down[f + 1][t])
        return 0

    lax.fori_loop(0, members // 8, block, 0)


def early_kernel(width, n, shift, rows, state, out):
    members = out.shape[0]
    tiles = state.shape[1] // members // rows
    q = owner_of(lax.axis_index("member"), shift, n)
    per = LANES // width
    lane = lax.broadcasted_iota(jnp.int32, (members, LANES), 1)
    slot = lane // width

    def line(f, r, tile):
        return state[f, pl.ds(tile * rows + r, members, stride=rows * tiles), :]

    tile = q * width // LANES
    offset = q * width - tile * LANES
    left = jnp.maximum(q * width - HALO, 0)
    right = jnp.minimum(q * width + width, tiles * LANES - HALO)
    left_tile, right_tile = left // LANES, right // LANES
    left_off, right_off = left - left_tile * LANES, right - right_tile * LANES
    has_left, has_right = q > 0, q < n - 1
    total = None
    for g in range(3 * rows):
        f, r = g // rows, g % rows
        i = r % per
        piece = pltpu.roll(line(f, r, tile), lax.rem(i * width - offset + LANES, LANES), 1)
        body = piece if i == 0 else jnp.where(slot == i, piece, body)
        if i == per - 1:
            out[:, pl.ds((g - i) * width, LANES)] = body
        at = g * 2 * HALO % LANES
        if at == 0:
            total = jnp.zeros((members, LANES), F32)
        piece = pltpu.roll(line(f, r, left_tile), lax.rem(at - left_off + LANES, LANES), 1)
        total = jnp.where((lane >= at) & (lane < at + HALO) & has_left, piece, total)
        at = at + HALO
        piece = pltpu.roll(line(f, r, right_tile), lax.rem(at - right_off + LANES, LANES), 1)
        total = jnp.where((lane >= at) & (lane < at + HALO) & has_right, piece, total)
        if at + HALO == LANES or g == 3 * rows - 1:
            first = 3 * rows * width + g * 2 * HALO // LANES * LANES
            out[:, pl.ds(first, LANES)] = total


def owner_model_kernel(width, n, rows, block_in, own, to_pair, to_cross):
    members = own.shape[0]
    per = LANES // width
    q = lax.axis_index("member")
    even = lax.axis_index("lat") % 2 == 0
    inside, spins = coefficients(rows)
    lane = lax.broadcasted_iota(jnp.int32, (8, LANES), 1)
    slot = lane // width
    middle = (LANES + width) // 2
    mine = (lane < width).astype(F32)
    on_right = ((lane >= width) & (lane < middle)).astype(F32) * (q < n - 1).astype(F32)
    on_left = (lane >= middle).astype(F32) * (q > 0).astype(F32)
    keep = mine + on_right + on_left

    def diff_lon(x):
        return [pltpu.roll(t, LANES - 1, 1) - pltpu.roll(t, 1, 1) for t in x]

    def dense(lines):
        total = lines[0]
        for i in range(1, per):
            total = jnp.where(slot == i, pltpu.roll(lines[i], i * width, 1), total)
        return total

    def block(b, _):
        at = pl.ds(pl.multiple_of(b * 8, 8), 8)
        base = {r: [None] * 3 for r in range(rows)}
        for g in range(3 * rows):
            f, r = g // rows, g % rows
            i = r % per
            body = block_in[at, pl.ds((g - i) * width, LANES)]
            if i:
                body = pltpu.roll(body, LANES - i * width, 1)
            place = g * 2 * HALO
            edge = block_in[at, pl.ds(3 * rows * width + place // LANES * LANES, LANES)]
            place = place % LANES
            left = pltpu.roll(edge, (LANES - HALO - place) % LANES, 1)
            right = pltpu.roll(edge, (width - HALO - place) % LANES, 1)
            row = jnp.where(lane < width, body, 0.0)
            row = jnp.where((lane >= width) & (lane < width + HALO), right, row)
            base[r][f] = [jnp.where(lane >= LANES - HALO, left, row)]
        y = integrate(base, diff_lon, keep, rows, inside, spins)
        for f in range(3):
            for r in range(0, rows, per):
                lines = [y[r + i][f][0] for i in range(per)]
                own[at, pl.ds((f * rows + r) * width, LANES)] = dense(lines)
            for i in range(0, HALO, per):
                up = dense([y[i + j - HALO][f][0] for j in range(per)])
                down = dense([y[rows + i + j][f][0] for j in range(per)])
                cols = pl.ds((f * HALO + i) * width, LANES)
                to_pair[at, cols] = jnp.where(even, down, up)
                to_cross[at, cols] = jnp.where(even, up, down)
        return 0

    lax.fori_loop(0, members // 8, block, 0)


def halo_places(rows):
    even = lax.axis_index("lat") % 2 == 0
    pair = jnp.where(even, rows - HALO, 0)
    return pair, rows - HALO - pair


def pick(array, lat, q):
    rows = array[lat].astype(F32)
    chosen = lax.broadcasted_iota(jnp.int32, rows.shape, 0) == q
    return jnp.sum(jnp.where(chosen, rows, 0.0), axis=0, keepdims=True)


def observe_kernel(width, own, got_pair, got_cross, cells, seen, height):
    _, rows, members, lon = own.shape
    patches, _, n_obs = seen.shape
    pair, cross = halo_places(rows)
    height[...] = own[0]
    height[pl.ds(pair, HALO)] += got_pair[...]
    height[pl.ds(cross, HALO)] += got_cross[...]
    for q in range(patches):
        start = q * width // LANES * LANES
        window = pl.ds(start, LANES)
        picked = pick(cells, lax.axis_index("lat"), q)
        for c in range(0, n_obs, LANES):
            cell = picked[:, c : c + LANES]
            row = jnp.floor((cell + 0.5) * (1.0 / width))
            lane = (cell - row * width).astype(jnp.int32) + (q * width - start)
            lane = jnp.broadcast_to(lane, (members, LANES))
            row = jnp.broadcast_to(row.astype(jnp.int32), (members, LANES))
            total = None
            for r in range(rows):
                taken = jnp.take_along_axis(height[r, :, window], lane, axis=1)
                total = taken if total is None else jnp.where(row == r, taken, total)
            seen[q, :, pl.ds(c, LANES)] = total


def pack_kernel(width, n, shifts, own, height, got_pair, got_cross, *refs):
    *outs, wind = refs
    _, rows, members, lon = own.shape
    pair, cross = halo_places(rows)
    wind[...] = own[1:3]
    for f in range(2):
        wind[f, pl.ds(pair, HALO)] += got_pair[f]
        wind[f, pl.ds(cross, HALO)] += got_cross[f]
    mine = lax.axis_index("member")
    per = LANES // width
    slot = lax.broadcasted_iota(jnp.int32, (members, LANES), 1) // width
    for s, out in zip(shifts, outs):
        q = owner_of(mine, s, n)
        start = pl.multiple_of(q * width // LANES * LANES, LANES)
        offset = q * width - start
        for f in range(3):
            source = height if f == 0 else wind.at[f - 1]
            for r in range(0, rows, per):
                total = None
                for i in range(per):
                    line = source[r + i, :, pl.ds(start, LANES)]
                    line = pltpu.roll(line, lax.rem(i * width - offset + LANES, LANES), 1)
                    total = line if total is None else jnp.where(slot == i, line, total)
                out[:, pl.ds((f * rows + r) * width, LANES)] = total


def owner_of(mine, shift, n):
    if n & (n - 1) == 0:
        return mine ^ shift
    return lax.rem(mine + shift, n)


def source_of(mine, shift, n):
    if n & (n - 1) == 0:
        return mine ^ shift
    return lax.rem(mine - shift + n, n)


def swap_links(n, shift):
    return [(i, owner_of(i, shift, n) if n & (n - 1) == 0 else (i + shift) % n) for i in range(n)]


def neighbour_links(n, first):
    links = [(i, i + 1) for i in range(first, n - 1, 2)]
    return links + [(j, i) for i, j in links]


def centred(raw):
    mean = jnp.sum(raw, axis=0, keepdims=True) * (1.0 / raw.shape[0])
    return raw - mean, mean


def gram_kernel(which, n, rows, width, cells, values, precs, raw_own, raw_pair, raw_cross, *outs):
    members, n_obs = raw_own.shape
    lat, mine = lax.axis_index("lat"), lax.axis_index("member")
    side = 1 - 2 * lax.rem(mine, 2)
    toward = 1 - 2 * lax.rem(lat, 2)
    total = [None] * len(which)
    for raw, b in ((raw_own, 0 * side), (raw_pair, side), (raw_cross, -side)):
        q = mine + b
        cell = pick(cells, lat, q)
        row = jnp.floor((cell + 0.5) * (1.0 / width))
        col = cell - row * width + (b * width).astype(F32)
        east = (col - 0.5 * (width - 1)) / width
        prec = pick(precs, lat, q)
        dev, mean = centred(raw[...])
        innovation = pick(values, lat, q) - mean
        right = split(dev)
        for i, t in enumerate(which):
            north = (row - (t * toward * rows).astype(F32) - 0.5 * (rows - 1)) / rows
            w = prec * jnp.exp(-0.5 * (north * north + east * east))
            left = jnp.concatenate(
                [dev * w, jnp.broadcast_to(innovation * w, (16, n_obs))], axis=0
            )
            part = dot3(split(left), right, (((1,), (1,)), ((), ())))
            total[i] = part if total[i] is None else total[i] + part
    for out, t in zip(outs, total):
        out[...] = t


def weights_kernel(own, got_pair, got_cross, out):
    members = own.shape[1]
    rows = lax.broadcasted_iota(jnp.int32, (members, members), 0)
    cols = lax.broadcasted_iota(jnp.int32, (members, members), 1)
    diagonal = rows == cols
    at = pl.ds(0, members)
    gram = own[at] + got_pair[at] + got_cross[at]
    gram = gram + jnp.where(diagonal, members - 1.0, 0.0)
    at = pl.ds(members, 8)
    drive = own[at] + got_pair[at] + got_cross[at]
    square = jnp.sum(jnp.sum(gram * gram, axis=0, keepdims=True), axis=1, keepdims=True)
    fro = jnp.sqrt(square)
    root = gram / fro
    inverse = None
    for sweep in range(ITERS):
        root_s = split(root)
        if inverse is None:
            product = root
        else:
            inverse_s = split(inverse)
            product = dot3(inverse_s, root_s)
        correction = jnp.where(diagonal, 1.5, 0.0) - 0.5 * product
        correction_s = split(correction)
        if sweep + 1 < ITERS:
            root = dot3(root_s, correction_s)
        inverse = correction if inverse is None else dot3(correction_s, inverse_s)
    inverse_s = split(inverse)
    mean_weight = dot3(split(dot3(split(drive), inverse_s)), inverse_s)[0:1] / fro
    weights = jnp.sqrt(members - 1.0) / jnp.sqrt(fro) * inverse + mean_weight
    sums = jnp.sum(weights, axis=1, keepdims=True)
    out[...] = weights + (1.0 - sums) * (1.0 / members)


def apply_kernel(n, shifts, early, rows, weights, *refs):
    parts, late, (pair_in, cross_in), outs, whole = (
        refs[: n - 1],
        refs[n - 1],
        refs[n : n + 2],
        refs[n + 2 : 2 * n + 2],
        refs[2 * n + 2],
    )
    local, cells = late.shape
    mine = lax.axis_index("member")

    def place(s):
        return pl.ds(pl.multiple_of(source_of(mine, s, n) * local, local), local)

    for s, part in zip(shifts, parts):
        whole[place(s), :] = part[...]
    at = place(early)
    whole[at, :] = late[...]
    edge = cells // 3 // rows * HALO
    for f in range(3):
        for got, first in zip((pair_in, cross_in), halo_places(rows)):
            start = pl.multiple_of(f * (cells // 3) + first // HALO * edge, edge)
            whole[at, pl.ds(start, edge)] += got[:, pl.ds(f * edge, edge)]
    wide = 2 * LANES
    for c in range(0, cells, wide):
        at = pl.ds(c, wide)
        field = split(whole[:, at])
        for s, out in enumerate(outs):
            k = pl.multiple_of(source_of(mine, s, n) * local, local)
            out[:, at] = dot3(split(weights[pl.ds(k, local), :]), field)


def unpack_kernel(width, n, rows, *refs):
    *parts, out, whole = refs
    members = parts[0].shape[0]
    mine = lax.axis_index("member")
    for s, part in enumerate(parts):
        whole[owner_of(mine, s, n)] = part[...]
    per = LANES // width
    tiles = n // per
    slot = lax.broadcasted_iota(jnp.int32, (members, LANES), 1) // width
    for f in range(3):
        for r in range(0, rows, per):
            cols = pl.ds((f * rows + r) * width, LANES)
            for t in range(tiles):
                lines = [whole[t * per + i, :, cols] for i in range(per)]
                for j in range(per):
                    total = None
                    for i in range(per):
                        line = lines[i]
                        if i != j:
                            line = pltpu.roll(line, (i - j) * width % LANES, 1)
                        total = line if total is None else jnp.where(slot == i, line, total)
                    out[f, pl.ds(t * rows + r + j, members, stride=rows * tiles), :] = total


def after(array, *others):
    return lax.optimization_barrier((array,) + others)[0]


def body(ensemble_state, obs_cell, obs_value, obs_prec):
    _, members, rows, lon = ensemble_state.shape
    n_lat, n_member = lax.axis_size("lat"), lax.axis_size("member")
    width = lon // n_member
    all_members = members * n_member
    n_obs = obs_cell.shape[2]
    pair_lat, cross_lat = neighbour_links(n_lat, 0), neighbour_links(n_lat, 1)
    pair_lon, cross_lon = neighbour_links(n_member, 0), neighbour_links(n_member, 1)

    tiles = lon // LANES
    state = ensemble_state.reshape(3, members, rows, tiles, LANES).transpose(0, 1, 3, 2, 4)
    state = state.reshape(3, members * tiles * rows, LANES)
    early = n_member // 2
    order = sorted(range(1, n_member), key=lambda s: (-(s & -s), s))
    late = [0] + [s for s in order if s != early]
    dense = 3 * rows * width
    halo_lanes = -(-3 * rows * 2 * HALO // LANES) * LANES
    (early_block,) = call(
        functools.partial(early_kernel, width, n_member, early, rows),
        ([(members, dense + halo_lanes)], []),
        state,
        name="early",
    )
    state = after(state, early_block)
    early_block = lax.ppermute(early_block, "member", swap_links(n_member, early))
    edge = (HALO, members, lon)
    own, h_pair, h_cross, uv_pair, uv_cross = call(
        model_kernel,
        ([(3, rows, members, lon), edge, edge, (2,) + edge, (2,) + edge], []),
        state,
        name="model",
    )
    got_cross = lax.ppermute(h_cross, "lat", cross_lat)
    got_pair = lax.ppermute(h_pair, "lat", pair_lat)
    seen, height = call(
        functools.partial(observe_kernel, width),
        ([(n_member, members, n_obs), (rows, members, lon)], []),
        own, got_pair, got_cross, obs_cell,
        name="observe",
    )
    seen = lax.all_to_all(seen, "member", split_axis=0, concat_axis=0, tiled=True)
    uv_cross = lax.ppermute(after(uv_cross, early_block), "lat", cross_lat)
    uv_pair = lax.ppermute(after(uv_pair, early_block), "lat", pair_lat)
    packed = call(
        functools.partial(pack_kernel, width, n_member, late),
        ([(members, dense)] * (n_member - 1), [pltpu.VMEM((2, rows, members, lon), F32)]),
        own, height, uv_pair, uv_cross,
        name="pack",
    )
    parts = [packed[0]] + [
        lax.ppermute(block, "member", swap_links(n_member, s))
        for s, block in zip(late[1:], packed[1:])
    ]
    beside = (members, 3 * HALO * width)
    early_own, early_pair, early_cross = call(
        functools.partial(owner_model_kernel, width, n_member, rows),
        ([(members, dense), beside, beside], []),
        early_block,
        name="owner_model",
    )
    early_cross = lax.ppermute(early_cross, "lat", cross_lat)
    early_pair = lax.ppermute(early_pair, "lat", pair_lat)
    raw = after(seen, early_block).reshape(all_members, n_obs)
    raw_cross = lax.ppermute(raw, "member", cross_lon)
    raw_pair = lax.ppermute(raw, "member", pair_lon)
    raw_cross, raw_pair = lax.optimization_barrier((raw_cross, raw_pair, *packed, early_own))[:2]
    gram_shape = (all_members + 16, all_members)
    sizes, observations = (n_member, rows, width), (obs_cell, obs_value, obs_prec)
    flops = 2 * 9 * all_members**2 * n_obs
    gram_cross, gram_pair = call(
        functools.partial(gram_kernel, (-1, 1), *sizes),
        ([gram_shape] * 2, []),
        *observations, raw, raw_pair, raw_cross,
        name="gram_beside", flops=2 * flops,
    )
    gram_cross = lax.ppermute(gram_cross, "lat", cross_lat)
    gram_pair = lax.ppermute(gram_pair, "lat", pair_lat)
    (gram_own,) = call(
        functools.partial(gram_kernel, (0,), *sizes),
        ([gram_shape], []),
        *observations, raw, raw_pair, raw_cross,
        name="gram_own", flops=flops,
    )
    (weights,) = call(
        weights_kernel,
        ([(all_members, all_members)], []),
        gram_own, gram_pair, gram_cross,
        name="weights", flops=2 * 9 * 12 * all_members**3,
    )
    shape = (members, dense)
    done = call(
        functools.partial(apply_kernel, n_member, late, early, rows),
        ([shape] * n_member, [pltpu.VMEM((all_members, dense), F32)]),
        weights, *parts, early_own, early_pair, early_cross,
        name="apply", flops=6 * all_members**2 * dense,
    )
    final = [done[0]] + [None] * (n_member - 1)
    for s in order:
        back = [(j, i) for i, j in swap_links(n_member, s)]
        final[s] = lax.ppermute(done[s], "member", back)
    (analysis,) = call(
        functools.partial(unpack_kernel, width, n_member, rows),
        ([(3, members * tiles * rows, LANES)], [pltpu.VMEM((n_member,) + shape, F32)]),
        *final,
        name="unpack",
    )
    analysis = analysis.reshape(3, members, tiles, rows, LANES).transpose(0, 1, 3, 2, 4)
    return analysis.reshape(ensemble_state.shape)


def solution(mesh):
    in_specs = (P(None, "member", "lat", None), P(), P(), P())
    out_specs = P(None, "member", "lat", None)
    return jax.shard_map(body, mesh=mesh, in_specs=in_specs, out_specs=out_specs, check_vma=False)
```

```python
import functools

import jax
import jax.numpy as jnp
from jax import lax
from jax.experimental import pallas as pl
from jax.experimental.pallas import tpu as pltpu
from jax.sharding import PartitionSpec as P

ITERS = 12
STEPS = 2
HALO = 2 * STEPS
LANES = 128
LIMIT = 12

time_step = 0.3
coriolis_base = 0.5
coriolis_slope = 1.0

F32 = jnp.float32
BF16 = jnp.bfloat16


def call(kernel, outs, *args, name, flops=0, limit=LIMIT, far_out=False):
    shapes = [jax.ShapeDtypeStruct(s, F32) for s in outs[0]]
    bytes_moved = 0
    return pl.pallas_call(
        kernel,
        out_shape=shapes,
        in_specs=[pl.BlockSpec(memory_space=pltpu.VMEM)] * len(args),
        out_specs=[pl.BlockSpec(memory_space=pl.ANY if far_out else pltpu.VMEM)] * len(shapes),
        scratch_shapes=outs[1],
        compiler_params=pltpu.CompilerParams(vmem_limit_bytes=limit * 2**20),
        cost_estimate=pl.CostEstimate(flops=0, bytes_accessed=bytes_moved, transcendentals=0),
        name=name,
    )(*args)


def split(x):
    high = x.astype(BF16)
    return high, (x - high.astype(F32)).astype(BF16)


def dot3(a, b, dims=(((1,), (0,)), ((), ()))):
    ah, al = a
    bh, bl = b
    dot = functools.partial(lax.dot_general, dimension_numbers=dims, preferred_element_type=F32)
    rows = ah.shape[0]
    both = dot(jnp.concatenate([ah, al], axis=0), bh)
    return both[:rows] + (both[rows:] + dot(ah, bl))


def coefficients(rows):
    lat, size = lax.axis_index("lat"), lax.axis_size("lat")
    inside_up = (lat > 0).astype(F32)
    inside_down = (lat < size - 1).astype(F32)
    inside = {r: inside_up if r < 0 else inside_down for r in range(-HALO, rows + HALO)}
    spins = {
        r: coriolis_base + coriolis_slope * ((lat * rows + r).astype(F32) / float(rows * size) - 0.5)
        for r in inside
    }
    return inside, spins


def integrate(base, diff_lon, keep, rows, inside, spins):
    tiles = len(base[0][0])
    y = dict(base)
    for step, factor in enumerate((time_step / 4, time_step / 2, time_step, 2 * time_step)):
        new = {}
        for r in range(-step - 1, rows + step + 1):
            scale = factor if 0 <= r < rows else factor * inside[r]
            half, turn = 0.5 * scale, scale * spins[r]
            if keep is not None:
                half, turn = half * keep, turn * keep
            here, below, above = y.get(r), y.get(r - 1), y.get(r + 1)
            rates = [[None] * tiles for _ in range(3)]

            def add(f, t, term):
                rates[f][t] = term if rates[f][t] is None else rates[f][t] + term

            if here is not None:
                slope_h, slope_u = diff_lon(here[0]), diff_lon(here[1])
            for t in range(tiles):
                d_v = d_h = None
                if above is not None and below is not None:
                    d_h, d_v = above[0][t] - below[0][t], above[2][t] - below[2][t]
                elif above is not None:
                    d_h, d_v = above[0][t], above[2][t]
                elif below is not None:
                    d_h, d_v = -below[0][t], -below[2][t]
                if here is not None:
                    d_v = slope_u[t] if d_v is None else d_v + slope_u[t]
                    add(1, t, turn * here[2][t] - half * slope_h[t])
                if d_v is not None:
                    add(0, t, -half * d_v)
                if d_h is not None:
                    add(2, t, -half * d_h)
                if here is not None:
                    add(2, t, -turn * here[1][t])
            for f in range(3):
                for t in range(tiles):
                    if r in base:
                        rates[f][t] = base[r][f][t] + rates[f][t]
                    elif rates[f][t] is None:
                        rates[f][t] = jnp.zeros((8, LANES), F32)
            new[r] = rates
        y = new
    return y


def model_kernel(state, own, h_pair, h_cross, uv_pair, uv_cross):
    _, rows, members, lon = own.shape
    tiles = lon // LANES
    even = lax.axis_index("lat") % 2 == 0
    inside, spins = coefficients(rows)
    lane = lax.broadcasted_iota(jnp.int32, (8, LANES), 1)
    first, last = lane == 0, lane == LANES - 1

    def diff_lon(x):
        right = [pltpu.roll(t, 1, 1) for t in x]
        left = [pltpu.roll(t, LANES - 1, 1) for t in x]
        out = []
        for t in range(tiles):
            before = jnp.where(first, right[t - 1] if t else 0.0, right[t])
            after = jnp.where(last, left[t + 1] if t + 1 < tiles else 0.0, left[t])
            out.append(after - before)
        return out

    def block(b, _):
        start = pl.multiple_of(b * 8, 8)

        def load(f, r):
            return [
                state[f, pl.ds((start * tiles + t) * rows + r, 8, stride=rows * tiles), :]
                for t in range(tiles)
            ]

        base = {r: [load(f, r) for f in range(3)] for r in range(rows)}
        y = integrate(base, diff_lon, None, rows, inside, spins)
        at = pl.ds(start, 8)
        for t in range(tiles):
            cols = pl.ds(t * LANES, LANES)
            for r in range(rows):
                for f in range(3):
                    own[f, r, at, cols] = y[r][f][t]
            for i in range(HALO):
                up, down = y[i - HALO], y[rows + i]
                h_pair[i, at, cols] = jnp.where(even, down[0][t], up[0][t])
                h_cross[i, at, cols] = jnp.where(even, up[0][t], down[0][t])
                for f in range(2):
                    uv_pair[f, i, at, cols] = jnp.where(even, down[f + 1][t], up[f + 1][t])
                    uv_cross[f, i, at, cols] = jnp.where(even, up[f + 1][t], down[f + 1][t])
        return 0

    lax.fori_loop(0, members // 8, block, 0, unroll=2)


def early_kernel(width, n, shift, rows, state, out):
    members = out.shape[0]
    tiles = state.shape[1] // members // rows
    q = owner_of(lax.axis_index("member"), shift, n)
    per = LANES // width
    lane = lax.broadcasted_iota(jnp.int32, (members, LANES), 1)
    slot = lane // width

    def line(f, r, tile):
        return state[f, pl.ds(tile * rows + r, members, stride=rows * tiles), :]

    tile = q * width // LANES
    offset = q * width - tile * LANES
    left = jnp.maximum(q * width - HALO, 0)
    right = jnp.minimum(q * width + width, tiles * LANES - HALO)
    left_tile, right_tile = left // LANES, right // LANES
    left_off, right_off = left - left_tile * LANES, right - right_tile * LANES
    has_left, has_right = q > 0, q < n - 1
    total = None
    for g in range(3 * rows):
        f, r = g // rows, g % rows
        i = r % per
        piece = pltpu.roll(line(f, r, tile), lax.rem(i * width - offset + LANES, LANES), 1)
        body = piece if i == 0 else jnp.where(slot == i, piece, body)
        if i == per - 1:
            out[:, pl.ds((g - i) * width, LANES)] = body
        at = g * 2 * HALO % LANES
        if at == 0:
            total = jnp.zeros((members, LANES), F32)
        piece = pltpu.roll(line(f, r, left_tile), lax.rem(at - left_off + LANES, LANES), 1)
        total = jnp.where((lane >= at) & (lane < at + HALO) & has_left, piece, total)
        at = at + HALO
        piece = pltpu.roll(line(f, r, right_tile), lax.rem(at - right_off + LANES, LANES), 1)
        total = jnp.where((lane >= at) & (lane < at + HALO) & has_right, piece, total)
        if at + HALO == LANES or g == 3 * rows - 1:
            first = 3 * rows * width + g * 2 * HALO // LANES * LANES
            out[:, pl.ds(first, LANES)] = total


def owner_model_kernel(width, n, rows, block_in, own, to_pair, to_cross):
    members = own.shape[0]
    per = LANES // width
    q = lax.axis_index("member")
    even = lax.axis_index("lat") % 2 == 0
    inside, spins = coefficients(rows)
    lane = lax.broadcasted_iota(jnp.int32, (8, LANES), 1)
    slot = lane // width
    middle = (LANES + width) // 2
    mine = (lane < width).astype(F32)
    on_right = ((lane >= width) & (lane < middle)).astype(F32) * (q < n - 1).astype(F32)
    on_left = (lane >= middle).astype(F32) * (q > 0).astype(F32)
    keep = mine + on_right + on_left

    def diff_lon(x):
        return [pltpu.roll(t, LANES - 1, 1) - pltpu.roll(t, 1, 1) for t in x]

    def dense(lines):
        total = lines[0]
        for i in range(1, per):
            total = jnp.where(slot == i, pltpu.roll(lines[i], i * width, 1), total)
        return total

    def block(b, _):
        at = pl.ds(pl.multiple_of(b * 8, 8), 8)
        base = {r: [None] * 3 for r in range(rows)}
        for g in range(3 * rows):
            f, r = g // rows, g % rows
            i = r % per
            body = block_in[at, pl.ds((g - i) * width, LANES)]
            if i:
                body = pltpu.roll(body, LANES - i * width, 1)
            place = g * 2 * HALO
            edge = block_in[at, pl.ds(3 * rows * width + place // LANES * LANES, LANES)]
            place = place % LANES
            left = pltpu.roll(edge, (LANES - HALO - place) % LANES, 1)
            right = pltpu.roll(edge, (width - HALO - place) % LANES, 1)
            row = jnp.where(lane < width, body, 0.0)
            row = jnp.where((lane >= width) & (lane < width + HALO), right, row)
            base[r][f] = [jnp.where(lane >= LANES - HALO, left, row)]
        y = integrate(base, diff_lon, keep, rows, inside, spins)
        for f in range(3):
            for r in range(0, rows, per):
                lines = [y[r + i][f][0] for i in range(per)]
                own[at, pl.ds((f * rows + r) * width, LANES)] = dense(lines)
            for i in range(0, HALO, per):
                up = dense([y[i + j - HALO][f][0] for j in range(per)])
                down = dense([y[rows + i + j][f][0] for j in range(per)])
                cols = pl.ds((f * HALO + i) * width, LANES)
                to_pair[at, cols] = jnp.where(even, down, up)
                to_cross[at, cols] = jnp.where(even, up, down)
        return 0

    lax.fori_loop(0, members // 8, block, 0, unroll=2)


def halo_places(rows):
    even = lax.axis_index("lat") % 2 == 0
    pair = jnp.where(even, rows - HALO, 0)
    return pair, rows - HALO - pair


def pick(array, lat, q):
    rows = array[lat].astype(F32)
    chosen = lax.broadcasted_iota(jnp.int32, rows.shape, 0) == q
    return jnp.sum(jnp.where(chosen, rows, 0.0), axis=0, keepdims=True)


def observe_kernel(width, own, got_pair, got_cross, cells, seen, height):
    _, rows, members, lon = own.shape
    patches, _, n_obs = seen.shape
    pair, cross = halo_places(rows)
    height[...] = own[0]
    height[pl.ds(pair, HALO)] += got_pair[...]
    height[pl.ds(cross, HALO)] += got_cross[...]
    for q in range(patches):
        start = q * width // LANES * LANES
        window = pl.ds(start, LANES)
        picked = pick(cells, lax.axis_index("lat"), q)
        for c in range(0, n_obs, LANES):
            cell = picked[:, c : c + LANES]
            row = jnp.floor((cell + 0.5) * (1.0 / width))
            lane = (cell - row * width).astype(jnp.int32) + (q * width - start)
            lane = jnp.broadcast_to(lane, (members, LANES))
            row = jnp.broadcast_to(row.astype(jnp.int32), (members, LANES))
            total = None
            for r in range(rows):
                taken = jnp.take_along_axis(height[r, :, window], lane, axis=1)
                total = taken if total is None else jnp.where(row == r, taken, total)
            seen[q, :, pl.ds(c, LANES)] = total


def pack_kernel(width, n, shifts, own, height, got_pair, got_cross, *refs):
    *outs, wind = refs
    _, rows, members, lon = own.shape
    pair, cross = halo_places(rows)
    wind[...] = own[1:3]
    for f in range(2):
        wind[f, pl.ds(pair, HALO)] += got_pair[f]
        wind[f, pl.ds(cross, HALO)] += got_cross[f]
    mine = lax.axis_index("member")
    per = LANES // width
    slot = lax.broadcasted_iota(jnp.int32, (members, LANES), 1) // width
    for s, out in zip(shifts, outs):
        q = owner_of(mine, s, n)
        start = pl.multiple_of(q * width // LANES * LANES, LANES)
        offset = q * width - start
        for f in range(3):
            source = height if f == 0 else wind.at[f - 1]
            for r in range(0, rows, per):
                total = None
                for i in range(per):
                    line = source[r + i, :, pl.ds(start, LANES)]
                    line = pltpu.roll(line, lax.rem(i * width - offset + LANES, LANES), 1)
                    total = line if total is None else jnp.where(slot == i, line, total)
                out[:, pl.ds((f * rows + r) * width, LANES)] = total


def owner_of(mine, shift, n):
    if n & (n - 1) == 0:
        return mine ^ shift
    return lax.rem(mine + shift, n)


def source_of(mine, shift, n):
    if n & (n - 1) == 0:
        return mine ^ shift
    return lax.rem(mine - shift + n, n)


def swap_links(n, shift):
    return [(i, owner_of(i, shift, n) if n & (n - 1) == 0 else (i + shift) % n) for i in range(n)]


def neighbour_links(n, first):
    links = [(i, i + 1) for i in range(first, n - 1, 2)]
    return links + [(j, i) for i, j in links]


def centred(raw):
    mean = jnp.sum(raw, axis=0, keepdims=True) * (1.0 / raw.shape[0])
    return raw - mean, mean


def gram_kernel(which, n, rows, width, cells, values, precs, raw_own, raw_pair, raw_cross, *outs):
    members, n_obs = raw_own.shape
    lat, mine = lax.axis_index("lat"), lax.axis_index("member")
    side = 1 - 2 * lax.rem(mine, 2)
    toward = 1 - 2 * lax.rem(lat, 2)
    total = [None] * len(which)
    for raw, b in ((raw_own, 0 * side), (raw_pair, side), (raw_cross, -side)):
        q = mine + b
        cell = pick(cells, lat, q)
        row = jnp.floor((cell + 0.5) * (1.0 / width))
        col = cell - row * width + (b * width).astype(F32)
        east = (col - 0.5 * (width - 1)) / width
        prec = pick(precs, lat, q)
        dev, mean = centred(raw[...])
        innovation = pick(values, lat, q) - mean
        right = split(dev)
        for i, t in enumerate(which):
            north = (row - (t * toward * rows).astype(F32) - 0.5 * (rows - 1)) / rows
            w = prec * jnp.exp(-0.5 * (north * north + east * east))
            left = jnp.concatenate(
                [dev * w, jnp.broadcast_to(innovation * w, (16, n_obs))], axis=0
            )
            part = dot3(split(left), right, (((1,), (1,)), ((), ())))
            total[i] = part if total[i] is None else total[i] + part
    for out, t in zip(outs, total):
        out[...] = t


def weights_kernel(own, got_pair, got_cross, out):
    members = own.shape[1]
    rows = lax.broadcasted_iota(jnp.int32, (members, members), 0)
    cols = lax.broadcasted_iota(jnp.int32, (members, members), 1)
    diagonal = rows == cols
    at = pl.ds(0, members)
    gram = own[at] + got_pair[at] + got_cross[at]
    gram = gram + jnp.where(diagonal, members - 1.0, 0.0)
    at = pl.ds(members, 8)
    drive = own[at] + got_pair[at] + got_cross[at]
    square = jnp.sum(jnp.sum(gram * gram, axis=0, keepdims=True), axis=1, keepdims=True)
    fro = jnp.sqrt(square)
    root = gram / fro
    inverse = None
    for sweep in range(ITERS):
        root_s = split(root)
        if inverse is None:
            product = root
        else:
            inverse_s = split(inverse)
            product = dot3(inverse_s, root_s)
        correction = jnp.where(diagonal, 1.5, 0.0) - 0.5 * product
        correction_s = split(correction)
        if sweep + 1 < ITERS:
            root = dot3(root_s, correction_s)
        inverse = correction if inverse is None else dot3(correction_s, inverse_s)
    inverse_s = split(inverse)
    mean_weight = dot3(split(dot3(split(drive), inverse_s)), inverse_s)[0:1] / fro
    weights = jnp.sqrt(members - 1.0) / jnp.sqrt(fro) * inverse + mean_weight
    sums = jnp.sum(weights, axis=1, keepdims=True)
    out[...] = weights + (1.0 - sums) * (1.0 / members)


def apply_kernel(n, shifts, early, rows, weights, *refs):
    parts, late, (pair_in, cross_in), outs, whole = (
        refs[: n - 1],
        refs[n - 1],
        refs[n : n + 2],
        refs[n + 2 : 2 * n + 2],
        refs[2 * n + 2],
    )
    local, cells = late.shape
    mine = lax.axis_index("member")

    def place(s):
        return pl.ds(pl.multiple_of(source_of(mine, s, n) * local, local), local)

    for s, part in zip(shifts, parts):
        whole[place(s), :] = part[...]
    at = place(early)
    whole[at, :] = late[...]
    edge = cells // 3 // rows * HALO
    for f in range(3):
        for got, first in zip((pair_in, cross_in), halo_places(rows)):
            start = pl.multiple_of(f * (cells // 3) + first // HALO * edge, edge)
            whole[at, pl.ds(start, edge)] += got[:, pl.ds(f * edge, edge)]
    wide = 2 * LANES
    for c in range(0, cells, wide):
        at = pl.ds(c, wide)
        field = split(whole[:, at])
        for s, out in enumerate(outs):
            k = pl.multiple_of(source_of(mine, s, n) * local, local)
            out[:, at] = dot3(split(weights[pl.ds(k, local), :]), field)


def unpack_kernel(width, n, rows, *refs):
    *parts, out, whole, done, sems = refs
    members = parts[0].shape[0]
    copies = []
    mine = lax.axis_index("member")
    for s, part in enumerate(parts):
        whole[owner_of(mine, s, n)] = part[...]
    per = LANES // width
    tiles = n // per
    slot = lax.broadcasted_iota(jnp.int32, (members, LANES), 1) // width
    for f in range(3):
        for r in range(0, rows, per):
            cols = pl.ds((f * rows + r) * width, LANES)
            for t in range(tiles):
                lines = [whole[t * per + i, :, cols] for i in range(per)]
                for j in range(per):
                    total = None
                    for i in range(per):
                        line = lines[i]
                        if i != j:
                            line = pltpu.roll(line, (i - j) * width % LANES, 1)
                        total = line if total is None else jnp.where(slot == i, line, total)
                    done[f, pl.ds(t * rows + r + j, members, stride=rows * tiles), :] = total
        copies.append(pltpu.make_async_copy(done.at[f], out.at[f], sems.at[f]))
        copies[-1].start()
    for copy in copies:
        copy.wait()


def after(array, *others):
    return lax.optimization_barrier((array,) + others)[0]


def body(ensemble_state, obs_cell, obs_value, obs_prec):
    _, members, rows, lon = ensemble_state.shape
    n_lat, n_member = lax.axis_size("lat"), lax.axis_size("member")
    width = lon // n_member
    all_members = members * n_member
    n_obs = obs_cell.shape[2]
    pair_lat, cross_lat = neighbour_links(n_lat, 0), neighbour_links(n_lat, 1)
    pair_lon, cross_lon = neighbour_links(n_member, 0), neighbour_links(n_member, 1)

    tiles = lon // LANES
    state = ensemble_state.reshape(3, members, rows, tiles, LANES).transpose(0, 1, 3, 2, 4)
    state = state.reshape(3, members * tiles * rows, LANES)
    early = n_member // 2
    order = sorted(range(1, n_member), key=lambda s: (-(s & -s), s))
    late = [0] + [s for s in order if s != early]
    dense = 3 * rows * width
    halo_lanes = -(-3 * rows * 2 * HALO // LANES) * LANES
    (early_block,) = call(
        functools.partial(early_kernel, width, n_member, early, rows),
        ([(members, dense + halo_lanes)], []),
        state,
        name="early",
    )
    state = after(state, early_block)
    early_block = lax.ppermute(early_block, "member", swap_links(n_member, early))
    edge = (HALO, members, lon)
    own, h_pair, h_cross, uv_pair, uv_cross = call(
        model_kernel,
        ([(3, rows, members, lon), edge, edge, (2,) + edge, (2,) + edge], []),
        state,
        name="model",
    )
    got_cross = lax.ppermute(h_cross, "lat", cross_lat)
    got_pair = lax.ppermute(h_pair, "lat", pair_lat)
    seen, height = call(
        functools.partial(observe_kernel, width),
        ([(n_member, members, n_obs), (rows, members, lon)], []),
        own, got_pair, got_cross, obs_cell,
        name="observe",
    )
    seen = lax.all_to_all(seen, "member", split_axis=0, concat_axis=0, tiled=True)
    uv_cross = lax.ppermute(after(uv_cross, early_block), "lat", cross_lat)
    uv_pair = lax.ppermute(after(uv_pair, early_block), "lat", pair_lat)
    packed = call(
        functools.partial(pack_kernel, width, n_member, late),
        ([(members, dense)] * (n_member - 1), [pltpu.VMEM((2, rows, members, lon), F32)]),
        own, height, uv_pair, uv_cross,
        name="pack",
    )
    parts = [packed[0]] + [
        lax.ppermute(block, "member", swap_links(n_member, s))
        for s, block in zip(late[1:], packed[1:])
    ]
    beside = (members, 3 * HALO * width)
    early_own, early_pair, early_cross = call(
        functools.partial(owner_model_kernel, width, n_member, rows),
        ([(members, dense), beside, beside], []),
        early_block,
        name="owner_model",
    )
    early_cross = lax.ppermute(early_cross, "lat", cross_lat)
    early_pair = lax.ppermute(early_pair, "lat", pair_lat)
    raw = after(seen, early_block).reshape(all_members, n_obs)
    raw_cross = lax.ppermute(raw, "member", cross_lon)
    raw_pair = lax.ppermute(raw, "member", pair_lon)
    raw_cross, raw_pair = lax.optimization_barrier((raw_cross, raw_pair, *packed, early_own))[:2]
    gram_shape = (all_members + 16, all_members)
    sizes, observations = (n_member, rows, width), (obs_cell, obs_value, obs_prec)
    flops = 2 * 9 * all_members**2 * n_obs
    gram_cross, gram_pair = call(
        functools.partial(gram_kernel, (-1, 1), *sizes),
        ([gram_shape] * 2, []),
        *observations, raw, raw_pair, raw_cross,
        name="gram_beside", flops=2 * flops,
    )
    gram_cross = lax.ppermute(gram_cross, "lat", cross_lat)
    gram_pair = lax.ppermute(gram_pair, "lat", pair_lat)
    raw_cross, raw_pair = lax.optimization_barrier((raw_cross, raw_pair, early_cross, early_pair))[:2]
    (gram_own,) = call(
        functools.partial(gram_kernel, (0,), *sizes),
        ([gram_shape], []),
        *observations, raw, raw_pair, raw_cross,
        name="gram_own", flops=flops,
    )
    (weights,) = call(
        weights_kernel,
        ([(all_members, all_members)], []),
        gram_own, gram_pair, gram_cross,
        name="weights", flops=2 * 9 * 12 * all_members**3,
    )
    shape = (members, dense)
    done = call(
        functools.partial(apply_kernel, n_member, late, early, rows),
        ([shape] * n_member, [pltpu.VMEM((all_members, dense), F32)]),
        weights, *parts, early_own, early_pair, early_cross,
        name="apply", flops=6 * all_members**2 * dense,
    )
    final = [done[0]] + [None] * (n_member - 1)
    for s in order:
        back = [(j, i) for i, j in swap_links(n_member, s)]
        final[s] = lax.ppermute(done[s], "member", back)
    (analysis,) = call(
        functools.partial(unpack_kernel, width, n_member, rows),
        (
            [(3, members * tiles * rows, LANES)],
            [
                pltpu.VMEM((n_member,) + shape, F32),
                pltpu.VMEM((3, members * tiles * rows, LANES), F32),
                pltpu.SemaphoreType.DMA((3,)),
            ],
        ),
        *final,
        name="unpack",
        far_out=True,
    )
    analysis = analysis.reshape(3, members, tiles, rows, LANES).transpose(0, 1, 3, 2, 4)
    return analysis.reshape(ensemble_state.shape)


def solution(mesh):
    in_specs = (P(None, "member", "lat", None), P(), P(), P())
    out_specs = P(None, "member", "lat", None)
    return jax.shard_map(body, mesh=mesh, in_specs=in_specs, out_specs=out_specs, check_vma=False)
```

```python
import functools

import jax
import jax.numpy as jnp
from jax import lax
from jax.experimental import pallas as pl
from jax.experimental.pallas import tpu as pltpu
from jax.sharding import PartitionSpec as P

ITERS = 12
STEPS = 2
HALO = 2 * STEPS
LANES = 128
LIMIT = 12

time_step = 0.3
coriolis_base = 0.5
coriolis_slope = 1.0

F32 = jnp.float32
BF16 = jnp.bfloat16


def call(kernel, outs, *args, name, flops=0, limit=LIMIT, far_out=False):
    shapes = [jax.ShapeDtypeStruct(s, F32) for s in outs[0]]
    bytes_moved = 0
    return pl.pallas_call(
        kernel,
        out_shape=shapes,
        in_specs=[pl.BlockSpec(memory_space=pltpu.VMEM)] * len(args),
        out_specs=[pl.BlockSpec(memory_space=pl.ANY if far_out else pltpu.VMEM)] * len(shapes),
        scratch_shapes=outs[1],
        compiler_params=pltpu.CompilerParams(vmem_limit_bytes=limit * 2**20),
        cost_estimate=pl.CostEstimate(flops=0, bytes_accessed=bytes_moved, transcendentals=0),
        name=name,
    )(*args)


def split(x):
    high = x.astype(BF16)
    return high, (x - high.astype(F32)).astype(BF16)


def dot3(a, b, dims=(((1,), (0,)), ((), ()))):
    ah, al = a
    bh, bl = b
    dot = functools.partial(lax.dot_general, dimension_numbers=dims, preferred_element_type=F32)
    rows = ah.shape[0]
    both = dot(jnp.concatenate([ah, al], axis=0), bh)
    return both[:rows] + (both[rows:] + dot(ah, bl))


def coefficients(rows):
    lat, size = lax.axis_index("lat"), lax.axis_size("lat")
    inside_up = (lat > 0).astype(F32)
    inside_down = (lat < size - 1).astype(F32)
    inside = {r: inside_up if r < 0 else inside_down for r in range(-HALO, rows + HALO)}
    spins = {
        r: coriolis_base + coriolis_slope * ((lat * rows + r).astype(F32) / float(rows * size) - 0.5)
        for r in inside
    }
    return inside, spins


def integrate(base, diff_lon, keep, rows, inside, spins):
    tiles = len(base[0][0])
    y = dict(base)
    for step, factor in enumerate((time_step / 4, time_step / 2, time_step, 2 * time_step)):
        new = {}
        for r in range(-step - 1, rows + step + 1):
            scale = factor if 0 <= r < rows else factor * inside[r]
            half, turn = 0.5 * scale, scale * spins[r]
            if keep is not None:
                half, turn = half * keep, turn * keep
            here, below, above = y.get(r), y.get(r - 1), y.get(r + 1)
            rates = [[None] * tiles for _ in range(3)]

            def add(f, t, term):
                rates[f][t] = term if rates[f][t] is None else rates[f][t] + term

            if here is not None:
                slope_h, slope_u = diff_lon(here[0]), diff_lon(here[1])
            for t in range(tiles):
                d_v = d_h = None
                if above is not None and below is not None:
                    d_h, d_v = above[0][t] - below[0][t], above[2][t] - below[2][t]
                elif above is not None:
                    d_h, d_v = above[0][t], above[2][t]
                elif below is not None:
                    d_h, d_v = -below[0][t], -below[2][t]
                if here is not None:
                    d_v = slope_u[t] if d_v is None else d_v + slope_u[t]
                    add(1, t, turn * here[2][t] - half * slope_h[t])
                if d_v is not None:
                    add(0, t, -half * d_v)
                if d_h is not None:
                    add(2, t, -half * d_h)
                if here is not None:
                    add(2, t, -turn * here[1][t])
            for f in range(3):
                for t in range(tiles):
                    if r in base:
                        rates[f][t] = base[r][f][t] + rates[f][t]
                    elif rates[f][t] is None:
                        rates[f][t] = jnp.zeros((8, LANES), F32)
            new[r] = rates
        y = new
    return y


def model_kernel(state, own, h_pair, h_cross, uv_pair, uv_cross):
    _, rows, members, lon = own.shape
    tiles = lon // LANES
    even = lax.axis_index("lat") % 2 == 0
    inside, spins = coefficients(rows)
    lane = lax.broadcasted_iota(jnp.int32, (8, LANES), 1)
    first, last = lane == 0, lane == LANES - 1

    def diff_lon(x):
        right = [pltpu.roll(t, 1, 1) for t in x]
        left = [pltpu.roll(t, LANES - 1, 1) for t in x]
        out = []
        for t in range(tiles):
            before = jnp.where(first, right[t - 1] if t else 0.0, right[t])
            after = jnp.where(last, left[t + 1] if t + 1 < tiles else 0.0, left[t])
            out.append(after - before)
        return out

    def block(b, _):
        start = pl.multiple_of(b * 8, 8)

        def load(f, r):
            return [
                state[f, pl.ds((start * tiles + t) * rows + r, 8, stride=rows * tiles), :]
                for t in range(tiles)
            ]

        base = {r: [load(f, r) for f in range(3)] for r in range(rows)}
        y = integrate(base, diff_lon, None, rows, inside, spins)
        at = pl.ds(start, 8)
        for t in range(tiles):
            cols = pl.ds(t * LANES, LANES)
            for r in range(rows):
                for f in range(3):
                    own[f, r, at, cols] = y[r][f][t]
            for i in range(HALO):
                up, down = y[i - HALO], y[rows + i]
                h_pair[i, at, cols] = jnp.where(even, down[0][t], up[0][t])
                h_cross[i, at, cols] = jnp.where(even, up[0][t], down[0][t])
                for f in range(2):
                    uv_pair[f, i, at, cols] = jnp.where(even, down[f + 1][t], up[f + 1][t])
                    uv_cross[f, i, at, cols] = jnp.where(even, up[f + 1][t], down[f + 1][t])
        return 0

    lax.fori_loop(0, members // 8, block, 0, unroll=2)


def early_kernel(width, n, shift, rows, state, out):
    members = out.shape[0]
    tiles = state.shape[1] // members // rows
    q = owner_of(lax.axis_index("member"), shift, n)
    per = LANES // width
    lane = lax.broadcasted_iota(jnp.int32, (members, LANES), 1)
    slot = lane // width

    def line(f, r, tile):
        return state[f, pl.ds(tile * rows + r, members, stride=rows * tiles), :]

    tile = q * width // LANES
    offset = q * width - tile * LANES
    left = jnp.maximum(q * width - HALO, 0)
    right = jnp.minimum(q * width + width, tiles * LANES - HALO)
    left_tile, right_tile = left // LANES, right // LANES
    left_off, right_off = left - left_tile * LANES, right - right_tile * LANES
    has_left, has_right = q > 0, q < n - 1
    total = None
    for g in range(3 * rows):
        f, r = g // rows, g % rows
        i = r % per
        piece = pltpu.roll(line(f, r, tile), lax.rem(i * width - offset + LANES, LANES), 1)
        body = piece if i == 0 else jnp.where(slot == i, piece, body)
        if i == per - 1:
            out[:, pl.ds((g - i) * width, LANES)] = body
        at = g * 2 * HALO % LANES
        if at == 0:
            total = jnp.zeros((members, LANES), F32)
        piece = pltpu.roll(line(f, r, left_tile), lax.rem(at - left_off + LANES, LANES), 1)
        total = jnp.where((lane >= at) & (lane < at + HALO) & has_left, piece, total)
        at = at + HALO
        piece = pltpu.roll(line(f, r, right_tile), lax.rem(at - right_off + LANES, LANES), 1)
        total = jnp.where((lane >= at) & (lane < at + HALO) & has_right, piece, total)
        if at + HALO == LANES or g == 3 * rows - 1:
            first = 3 * rows * width + g * 2 * HALO // LANES * LANES
            out[:, pl.ds(first, LANES)] = total


def owner_model_kernel(width, n, rows, block_in, own, to_pair, to_cross):
    members = own.shape[0]
    per = LANES // width
    q = lax.axis_index("member")
    even = lax.axis_index("lat") % 2 == 0
    inside, spins = coefficients(rows)
    lane = lax.broadcasted_iota(jnp.int32, (8, LANES), 1)
    slot = lane // width
    middle = (LANES + width) // 2
    mine = (lane < width).astype(F32)
    on_right = ((lane >= width) & (lane < middle)).astype(F32) * (q < n - 1).astype(F32)
    on_left = (lane >= middle).astype(F32) * (q > 0).astype(F32)
    keep = mine + on_right + on_left

    def diff_lon(x):
        return [pltpu.roll(t, LANES - 1, 1) - pltpu.roll(t, 1, 1) for t in x]

    def dense(lines):
        total = lines[0]
        for i in range(1, per):
            total = jnp.where(slot == i, pltpu.roll(lines[i], i * width, 1), total)
        return total

    def block(b, _):
        at = pl.ds(pl.multiple_of(b * 8, 8), 8)
        base = {r: [None] * 3 for r in range(rows)}
        for g in range(3 * rows):
            f, r = g // rows, g % rows
            i = r % per
            body = block_in[at, pl.ds((g - i) * width, LANES)]
            if i:
                body = pltpu.roll(body, LANES - i * width, 1)
            place = g * 2 * HALO
            edge = block_in[at, pl.ds(3 * rows * width + place // LANES * LANES, LANES)]
            place = place % LANES
            left = pltpu.roll(edge, (LANES - HALO - place) % LANES, 1)
            right = pltpu.roll(edge, (width - HALO - place) % LANES, 1)
            row = jnp.where(lane < width, body, 0.0)
            row = jnp.where((lane >= width) & (lane < width + HALO), right, row)
            base[r][f] = [jnp.where(lane >= LANES - HALO, left, row)]
        y = integrate(base, diff_lon, keep, rows, inside, spins)
        for f in range(3):
            for r in range(0, rows, per):
                lines = [y[r + i][f][0] for i in range(per)]
                own[at, pl.ds((f * rows + r) * width, LANES)] = dense(lines)
            for i in range(0, HALO, per):
                up = dense([y[i + j - HALO][f][0] for j in range(per)])
                down = dense([y[rows + i + j][f][0] for j in range(per)])
                cols = pl.ds((f * HALO + i) * width, LANES)
                to_pair[at, cols] = jnp.where(even, down, up)
                to_cross[at, cols] = jnp.where(even, up, down)
        return 0

    lax.fori_loop(0, members // 8, block, 0, unroll=2)


def halo_places(rows):
    even = lax.axis_index("lat") % 2 == 0
    pair = jnp.where(even, rows - HALO, 0)
    return pair, rows - HALO - pair


def pick(array, lat, q):
    rows = array[lat].astype(F32)
    chosen = lax.broadcasted_iota(jnp.int32, rows.shape, 0) == q
    return jnp.sum(jnp.where(chosen, rows, 0.0), axis=0, keepdims=True)


def observe_kernel(width, own, got_pair, got_cross, cells, seen, height):
    _, rows, members, lon = own.shape
    patches, _, n_obs = seen.shape
    pair, cross = halo_places(rows)
    height[...] = own[0]
    height[pl.ds(pair, HALO)] += got_pair[...]
    height[pl.ds(cross, HALO)] += got_cross[...]
    for q in range(patches):
        start = q * width // LANES * LANES
        window = pl.ds(start, LANES)
        picked = pick(cells, lax.axis_index("lat"), q)
        for c in range(0, n_obs, LANES):
            cell = picked[:, c : c + LANES]
            row = jnp.floor((cell + 0.5) * (1.0 / width))
            lane = (cell - row * width).astype(jnp.int32) + (q * width - start)
            lane = jnp.broadcast_to(lane, (members, LANES))
            row = jnp.broadcast_to(row.astype(jnp.int32), (members, LANES))
            total = None
            for r in range(rows):
                taken = jnp.take_along_axis(height[r, :, window], lane, axis=1)
                total = taken if total is None else jnp.where(row == r, taken, total)
            seen[q, :, pl.ds(c, LANES)] = total


def owner_blocks(width, n, shifts, fields, outs):
    rows, members, _ = fields[0].shape
    mine = lax.axis_index("member")
    per = LANES // width
    slot = lax.broadcasted_iota(jnp.int32, (members, LANES), 1) // width
    for s, out in zip(shifts, outs):
        q = owner_of(mine, s, n)
        start = pl.multiple_of(q * width // LANES * LANES, LANES)
        offset = q * width - start
        for f, field in enumerate(fields):
            for r in range(0, rows, per):
                total = None
                for i in range(per):
                    line = field[r + i, :, pl.ds(start, LANES)]
                    line = pltpu.roll(line, lax.rem(i * width - offset + LANES, LANES), 1)
                    total = line if total is None else jnp.where(slot == i, line, total)
                out[:, pl.ds((f * rows + r) * width, LANES)] = total


def pack_height_kernel(width, n, shifts, height, *outs):
    owner_blocks(width, n, shifts, [height], outs)


def pack_kernel(width, n, shifts, own, got_pair, got_cross, *refs):
    *outs, wind = refs
    pair, cross = halo_places(own.shape[1])
    wind[...] = own[1:3]
    for f in range(2):
        wind[f, pl.ds(pair, HALO)] += got_pair[f]
        wind[f, pl.ds(cross, HALO)] += got_cross[f]
    owner_blocks(width, n, shifts, [wind.at[0], wind.at[1]], outs)


def owner_of(mine, shift, n):
    if n & (n - 1) == 0:
        return mine ^ shift
    return lax.rem(mine + shift, n)


def source_of(mine, shift, n):
    if n & (n - 1) == 0:
        return mine ^ shift
    return lax.rem(mine - shift + n, n)


def swap_links(n, shift):
    return [(i, owner_of(i, shift, n) if n & (n - 1) == 0 else (i + shift) % n) for i in range(n)]


def neighbour_links(n, first):
    links = [(i, i + 1) for i in range(first, n - 1, 2)]
    return links + [(j, i) for i, j in links]


def centred(raw):
    mean = jnp.sum(raw, axis=0, keepdims=True) * (1.0 / raw.shape[0])
    return raw - mean, mean


def gram_kernel(which, n, rows, width, cells, values, precs, raw_own, raw_pair, raw_cross, *outs):
    members, n_obs = raw_own.shape
    lat, mine = lax.axis_index("lat"), lax.axis_index("member")
    side = 1 - 2 * lax.rem(mine, 2)
    toward = 1 - 2 * lax.rem(lat, 2)
    total = [None] * len(which)
    for raw, b in ((raw_own, 0 * side), (raw_pair, side), (raw_cross, -side)):
        q = mine + b
        cell = pick(cells, lat, q)
        row = jnp.floor((cell + 0.5) * (1.0 / width))
        col = cell - row * width + (b * width).astype(F32)
        east = (col - 0.5 * (width - 1)) / width
        prec = pick(precs, lat, q)
        dev, mean = centred(raw[...])
        innovation = pick(values, lat, q) - mean
        right = split(dev)
        for i, t in enumerate(which):
            north = (row - (t * toward * rows).astype(F32) - 0.5 * (rows - 1)) / rows
            w = prec * jnp.exp(-0.5 * (north * north + east * east))
            left = jnp.concatenate(
                [dev * w, jnp.broadcast_to(innovation * w, (16, n_obs))], axis=0
            )
            part = dot3(split(left), right, (((1,), (1,)), ((), ())))
            total[i] = part if total[i] is None else total[i] + part
    for out, t in zip(outs, total):
        out[...] = t


def weights_kernel(own, got_pair, got_cross, out):
    members = own.shape[1]
    rows = lax.broadcasted_iota(jnp.int32, (members, members), 0)
    cols = lax.broadcasted_iota(jnp.int32, (members, members), 1)
    diagonal = rows == cols
    at = pl.ds(0, members)
    gram = own[at] + got_pair[at] + got_cross[at]
    gram = gram + jnp.where(diagonal, members - 1.0, 0.0)
    at = pl.ds(members, 8)
    drive = own[at] + got_pair[at] + got_cross[at]
    square = jnp.sum(jnp.sum(gram * gram, axis=0, keepdims=True), axis=1, keepdims=True)
    fro = jnp.sqrt(square)
    root = gram / fro
    inverse = None
    for sweep in range(ITERS):
        root_s = split(root)
        if inverse is None:
            product = root
        else:
            inverse_s = split(inverse)
            product = dot3(inverse_s, root_s)
        correction = jnp.where(diagonal, 1.5, 0.0) - 0.5 * product
        correction_s = split(correction)
        if sweep + 1 < ITERS:
            root = dot3(root_s, correction_s)
        inverse = correction if inverse is None else dot3(correction_s, inverse_s)
    inverse_s = split(inverse)
    mean_weight = dot3(split(dot3(split(drive), inverse_s)), inverse_s)[0:1] / fro
    weights = jnp.sqrt(members - 1.0) / jnp.sqrt(fro) * inverse + mean_weight
    sums = jnp.sum(weights, axis=1, keepdims=True)
    out[...] = weights + (1.0 - sums) * (1.0 / members)


def apply_kernel(n, shifts, early, rows, weights, *refs):
    heights, parts = refs[: n - 1], refs[n - 1 : 2 * n - 2]
    late, pair_in, cross_in = refs[2 * n - 2 : 2 * n + 1]
    outs, whole = refs[2 * n + 1 : 3 * n + 1], refs[3 * n + 1]
    local, cells = late.shape
    mine = lax.axis_index("member")

    def place(s):
        return pl.ds(pl.multiple_of(source_of(mine, s, n) * local, local), local)

    for s, height, part in zip(shifts, heights, parts):
        whole[place(s), : cells // 3] = height[...]
        whole[place(s), cells // 3 :] = part[...]
    at = place(early)
    whole[at, :] = late[...]
    edge = cells // 3 // rows * HALO
    for f in range(3):
        for got, first in zip((pair_in, cross_in), halo_places(rows)):
            start = pl.multiple_of(f * (cells // 3) + first // HALO * edge, edge)
            whole[at, pl.ds(start, edge)] += got[:, pl.ds(f * edge, edge)]
    wide = 2 * LANES
    for c in range(0, cells, wide):
        at = pl.ds(c, wide)
        field = split(whole[:, at])
        for s, out in enumerate(outs):
            k = pl.multiple_of(source_of(mine, s, n) * local, local)
            out[:, at] = dot3(split(weights[pl.ds(k, local), :]), field)


def unpack_kernel(width, n, rows, *refs):
    *parts, out, whole, done, sems = refs
    members = parts[0].shape[0]
    copies = []
    mine = lax.axis_index("member")
    for s, part in enumerate(parts):
        whole[owner_of(mine, s, n)] = part[...]
    per = LANES // width
    tiles = n // per
    slot = lax.broadcasted_iota(jnp.int32, (members, LANES), 1) // width
    for f in range(3):
        for r in range(0, rows, per):
            cols = pl.ds((f * rows + r) * width, LANES)
            for t in range(tiles):
                lines = [whole[t * per + i, :, cols] for i in range(per)]
                for j in range(per):
                    total = None
                    for i in range(per):
                        line = lines[i]
                        if i != j:
                            line = pltpu.roll(line, (i - j) * width % LANES, 1)
                        total = line if total is None else jnp.where(slot == i, line, total)
                    done[f, pl.ds(t * rows + r + j, members, stride=rows * tiles), :] = total
        copies.append(pltpu.make_async_copy(done.at[f], out.at[f], sems.at[f]))
        copies[-1].start()
    for copy in copies:
        copy.wait()


def after(array, *others):
    return lax.optimization_barrier((array,) + others)[0]


def body(ensemble_state, obs_cell, obs_value, obs_prec):
    _, members, rows, lon = ensemble_state.shape
    n_lat, n_member = lax.axis_size("lat"), lax.axis_size("member")
    width = lon // n_member
    all_members = members * n_member
    n_obs = obs_cell.shape[2]
    pair_lat, cross_lat = neighbour_links(n_lat, 0), neighbour_links(n_lat, 1)
    pair_lon, cross_lon = neighbour_links(n_member, 0), neighbour_links(n_member, 1)

    tiles = lon // LANES
    state = ensemble_state.reshape(3, members, rows, tiles, LANES).transpose(0, 1, 3, 2, 4)
    state = state.reshape(3, members * tiles * rows, LANES)
    early = n_member // 2
    order = sorted(range(1, n_member), key=lambda s: (-(s & -s), s))
    late = [0] + [s for s in order if s != early]
    dense = 3 * rows * width
    halo_lanes = -(-3 * rows * 2 * HALO // LANES) * LANES
    (early_block,) = call(
        functools.partial(early_kernel, width, n_member, early, rows),
        ([(members, dense + halo_lanes)], []),
        state,
        name="early",
    )
    state = after(state, early_block)
    early_block = lax.ppermute(early_block, "member", swap_links(n_member, early))
    edge = (HALO, members, lon)
    own, h_pair, h_cross, uv_pair, uv_cross = call(
        model_kernel,
        ([(3, rows, members, lon), edge, edge, (2,) + edge, (2,) + edge], []),
        state,
        name="model",
    )
    got_cross = lax.ppermute(h_cross, "lat", cross_lat)
    got_pair = lax.ppermute(h_pair, "lat", pair_lat)
    seen, height = call(
        functools.partial(observe_kernel, width),
        ([(n_member, members, n_obs), (rows, members, lon)], []),
        own, got_pair, got_cross, obs_cell,
        name="observe",
    )
    seen = lax.all_to_all(seen, "member", split_axis=0, concat_axis=0, tiled=True)
    uv_cross = lax.ppermute(after(uv_cross, early_block), "lat", cross_lat)
    uv_pair = lax.ppermute(after(uv_pair, early_block), "lat", pair_lat)
    heights = call(
        functools.partial(pack_height_kernel, width, n_member, late),
        ([(members, rows * width)] * (n_member - 1), []),
        height,
        name="pack_height",
    )
    packed = call(
        functools.partial(pack_kernel, width, n_member, late),
        ([(members, 2 * rows * width)] * (n_member - 1), [pltpu.VMEM((2, rows, members, lon), F32)]),
        own, uv_pair, uv_cross,
        name="pack",
    )

    def to_owners(blocks):
        return [blocks[0]] + [
            lax.ppermute(block, "member", swap_links(n_member, s))
            for s, block in zip(late[1:], blocks[1:])
        ]

    heights, parts = to_owners(heights), to_owners(packed)
    beside = (members, 3 * HALO * width)
    early_own, early_pair, early_cross = call(
        functools.partial(owner_model_kernel, width, n_member, rows),
        ([(members, dense), beside, beside], []),
        early_block,
        name="owner_model",
    )
    early_cross = lax.ppermute(early_cross, "lat", cross_lat)
    early_pair = lax.ppermute(early_pair, "lat", pair_lat)
    raw = after(seen, early_block).reshape(all_members, n_obs)
    raw_cross = lax.ppermute(raw, "member", cross_lon)
    raw_pair = lax.ppermute(raw, "member", pair_lon)
    raw_cross, raw_pair = lax.optimization_barrier((raw_cross, raw_pair, *packed, early_own))[:2]
    gram_shape = (all_members + 16, all_members)
    sizes, observations = (n_member, rows, width), (obs_cell, obs_value, obs_prec)
    flops = 2 * 9 * all_members**2 * n_obs
    gram_cross, gram_pair = call(
        functools.partial(gram_kernel, (-1, 1), *sizes),
        ([gram_shape] * 2, []),
        *observations, raw, raw_pair, raw_cross,
        name="gram_beside", flops=2 * flops,
    )
    gram_cross = lax.ppermute(gram_cross, "lat", cross_lat)
    gram_pair = lax.ppermute(gram_pair, "lat", pair_lat)
    raw_cross, raw_pair = lax.optimization_barrier((raw_cross, raw_pair, early_cross, early_pair, *heights))[:2]
    (gram_own,) = call(
        functools.partial(gram_kernel, (0,), *sizes),
        ([gram_shape], []),
        *observations, raw, raw_pair, raw_cross,
        name="gram_own", flops=flops,
    )
    (weights,) = call(
        weights_kernel,
        ([(all_members, all_members)], []),
        gram_own, gram_pair, gram_cross,
        name="weights", flops=2 * 9 * 12 * all_members**3,
    )
    shape = (members, dense)
    done = call(
        functools.partial(apply_kernel, n_member, late, early, rows),
        ([shape] * n_member, [pltpu.VMEM((all_members, dense), F32)]),
        weights, *heights, *parts, early_own, early_pair, early_cross,
        name="apply", flops=6 * all_members**2 * dense,
    )
    final = [done[0]] + [None] * (n_member - 1)
    for s in sorted(range(1, n_member), key=lambda s: (s != early, -s)):
        back = [(j, i) for i, j in swap_links(n_member, s)]
        final[s] = lax.ppermute(done[s], "member", back)
    (analysis,) = call(
        functools.partial(unpack_kernel, width, n_member, rows),
        (
            [(3, members * tiles * rows, LANES)],
            [
                pltpu.VMEM((n_member,) + shape, F32),
                pltpu.VMEM((3, members * tiles * rows, LANES), F32),
                pltpu.SemaphoreType.DMA((3,)),
            ],
        ),
        *final,
        name="unpack",
        far_out=True,
    )
    analysis = analysis.reshape(3, members, tiles, rows, LANES).transpose(0, 1, 3, 2, 4)
    return analysis.reshape(ensemble_state.shape)


def solution(mesh):
    in_specs = (P(None, "member", "lat", None), P(), P(), P())
    out_specs = P(None, "member", "lat", None)
    return jax.shard_map(body, mesh=mesh, in_specs=in_specs, out_specs=out_specs, check_vma=False)
```
